32 devices in a mesh: seg: 2 (over y), rows: 8 (over z, x), cam: 2 (over core).
Axes of the slice: x: 2, y: 2, z: 4, core: 2. Of those that a mesh axis runs over, the one named last changes fastest.
Arguments:
- features: bfloat16 [4, 128, 32, 128], P(('seg', 'cam'), None, 'rows'), parts along dimension 0, may hold values from -6 to 6
- partner: int32 [2], replicated, may hold values from 0 to 1, as said below
- pattern: int32 [64, 6], P(('seg', 'rows')), parts along dimension 0, may hold values from 0 to 1, as said below
- valid: int32 [4, 32, 4], P(('seg', 'cam'), 'rows'), parts along dimension 0, may hold values 0 or 1
- carried: bfloat16 [4, 16, 96, 32, 128], P(('seg', 'cam'), None, None, 'rows'), parts along dimension 0, may hold values from -6 to 6
- w_first: bfloat16 [27, 16], replicated, may hold values from -1.25 to 1.25
- w_second: bfloat16 [27, 16, 16], replicated, may hold values from -0.3125 to 0.3125
- w_third: bfloat16 [27, 16, 16], replicated, may hold values from -0.3125 to 0.3125
- w_last: bfloat16 [27, 16], replicated, may hold values from -0.3125 to 0.3125
Outputs:
- aggregated: float32 [4, 96, 32, 128], P(('seg', 'cam'), None, 'rows'), parts along dimension 0
The draws below stay inside these ranges and needn't reach their ends.
There are 2 independent parts, one for each index of `seg`. The reference program is written for one: setup_inputs(seed, part) draws one part's arguments, and reference() takes and returns one part's arrays. A program takes and returns all parts, laid end to end along the dimension named above; an argument that names none is the same for every part. Nothing has to cross between parts.
Inputs may be any that keep to these rules, and one draw needn't show every extreme that they name: partner is its own inverse; cameras 0 to 0 pair with cameras 1 to 1. `pattern`: in every row the live tiles (ones) form one run of consecutive tiles, at least one.
All inputs are finite; a program needn't handle non-finite values. No bound on the sum of `valid` on one device may be relied on, other than what follows from the above.
Results may differ from the reference program's by a relative error of at most 0.0037.
Values may be sent and summed in bfloat16 or wider, within the bound.
No kernel may reach another device: no remote copies, remote signals or barrier semaphores. Data moves between devices by JAX's collectives and lax.ppermute only.
A program may use at most 128 MiB of HBM per device.

```python
import jax
import jax.numpy as jnp
from jax import lax

C = 128
DISP = 96
AGG = 16
DTILE = 16
BLOCK_COLS = 32
W = 128
CAM_DEV = 1
ROWS = 32
CAMS = 2
DTILES = 6
WBLOCKS = 4


def draw_partner(key, part):
    key = jax.random.fold_in(key, 5)
    order = jax.random.permutation(key, CAM_DEV)
    inverse = jnp.argsort(order)
    return jnp.concatenate([CAM_DEV + order, inverse]).astype(jnp.int32)


def draw_pattern(key, part):
    key = jax.random.fold_in(key, 11)
    first_key, span_key = jax.random.split(key)
    lowest = jax.random.randint(first_key, (ROWS, 1), 0, DTILES)
    spans = jax.random.randint(span_key, (ROWS, 1), 1, DTILES + 1)
    tiles = jnp.arange(DTILES)[None, :]
    return ((tiles >= lowest) & (tiles < lowest + spans)).astype(jnp.int32)


def with_ends(drawn, stream_key, low, high):
    index_at = [jax.random.randint(jax.random.fold_in(stream_key, axis), (), 0, length) for axis, length in enumerate(drawn.shape)]
    widest = drawn.shape.index(max(drawn.shape))
    next_to = index_at[:widest] + [(index_at[widest] + 1) % drawn.shape[widest]] + index_at[widest + 1:]
    return drawn.at[tuple(index_at)].set(low).at[tuple(next_to)].set(high)


def block_scale(key, dims, cuts, low, top_value):
    gain, own = 1.0, jax.random.fold_in(key, 6)
    for axis_at, shards_of in cuts:
        steps = jnp.exp(jax.random.uniform(jax.random.fold_in(own, axis_at), (shards_of,), jnp.float32, low / len(cuts), top_value / len(cuts)))
        gain = gain * jnp.repeat(steps, dims[axis_at] // shards_of).reshape([-1 if axis == axis_at else 1 for axis in range(len(dims))])
    return gain


def bell_draw(key, extent, spread, bound, pieces=(), kind=jnp.bfloat16):
    entries = spread * jax.random.normal(key, extent, jnp.float32)
    if pieces:
        entries = entries * block_scale(key, extent, pieces, -0.22, 0.18)
    return jnp.clip(entries, -bound, bound).astype(kind)


def setup_inputs(seed: int = 0, part: int = 0) -> dict:
    key_of = jax.random.split(jax.random.key(seed), 10)
    own_keys = jax.random.split(jax.random.fold_in(key_of[9], part), 10)
    features = bell_draw(own_keys[0], (CAMS, C, ROWS, W), 1.0, 6.0, ((0, 2), (2, 8)))
    partner = draw_partner(jax.random.fold_in(key_of[9], 71), part)
    pattern = draw_pattern(jax.random.fold_in(jax.random.fold_in(key_of[9], part), 71), part)
    valid = with_ends((jax.random.randint(own_keys[3], (CAMS, ROWS, WBLOCKS), 0, 8) < 7).astype(jnp.int32), jax.random.fold_in(own_keys[3], 1), 0, 1)
    carried = bell_draw(own_keys[4], (CAMS, AGG, DISP, ROWS, W), 1.0, 6.0, ((0, 2), (3, 8)))
    w_first = bell_draw(key_of[5], (27, AGG), 27 ** -0.5, 1.25)
    w_second = bell_draw(key_of[6], (27, AGG, AGG), (27 * AGG) ** -0.5, 0.3125)
    w_third = bell_draw(key_of[7], (27, AGG, AGG), (27 * AGG) ** -0.5, 0.3125)
    w_last = bell_draw(key_of[8], (27, AGG), (27 * AGG) ** -0.5, 0.3125)
    return dict(features=features, partner=partner, pattern=pattern, valid=valid, carried=carried, w_first=w_first, w_second=w_second, w_third=w_third, w_last=w_last)


def conv_all(x, kernel):
    outs, ins = (kernel.shape[1], kernel.shape[2])
    weights = kernel.astype(jnp.float32).reshape(3, 3, 3, outs, ins).transpose(3, 4, 0, 1, 2)
    return lax.conv_general_dilated(x.astype(jnp.float32), weights, (1, 1, 1), ((1, 1), (1, 1), (1, 1)), dimension_numbers=('NCDHW', 'OIDHW', 'NCDHW'), precision=lax.Precision.HIGHEST)

def reference(features, partner, pattern, valid, carried, w_first, w_second, w_third, w_last):
    idents = jnp.arange(CAMS, dtype=jnp.int32)
    right = (partner < idents)[:, None, None, None]
    own = jnp.where(right, features[..., ::-1], features).astype(jnp.float32)
    mate = features[partner]
    mate = jnp.where(right, mate[..., ::-1], mate)
    padded = jnp.pad(mate, ((0, 0), (0, 0), (0, 0), (DISP, 0))).astype(jnp.float32)

    def one_disp(shift):
        moved = lax.dynamic_slice_in_dim(padded, (DISP - shift).astype(jnp.int32), W, axis=3)
        return lax.optimization_barrier(jnp.sum(own * moved, axis=1))
    corr = lax.map(one_disp, jnp.arange(DISP, dtype=jnp.int32)).transpose(1, 0, 2, 3)
    corr = corr / jnp.sqrt(jnp.float32(C))
    corr = jnp.where(right, corr[..., ::-1], corr)
    tiles = jnp.repeat(pattern, DTILE, axis=1).T.astype(jnp.float32)
    pixels = jnp.repeat(valid, BLOCK_COLS, axis=2).astype(jnp.float32)
    corr = (corr * tiles[None, :, :, None] * pixels[:, None, :, :]).astype(jnp.bfloat16)
    volume = corr[:, None]
    h1 = jax.nn.relu(conv_all(volume, w_first[:, :, None])).astype(jnp.bfloat16)
    h2 = jax.nn.relu(conv_all(h1, w_second) + carried.astype(jnp.float32)).astype(jnp.bfloat16)
    h3 = jax.nn.relu(conv_all(h2, w_third)).astype(jnp.bfloat16)
    final = conv_all(h3, w_last[:, None, :])[:, 0]
    return corr.astype(jnp.float32) + final
```

```python
import numpy as np
import jax
import jax.numpy as jnp
from jax import lax
from jax.experimental import pallas as pl
from jax.experimental.pallas import tpu as pltpu
from jax.sharding import PartitionSpec as P

DTILE = 16
BLOCK_COLS = 32
BF = jnp.bfloat16
F32 = jnp.float32
VM = pl.BlockSpec(memory_space=pltpu.VMEM)
SM = pl.BlockSpec(memory_space=pltpu.SMEM)
MIB = 2**20

R, W, A = 4, 128, 16
T1 = 14


def window_starts(disp):
    count = -(-disp // T1)
    return [min(T1 * k, disp - T1) for k in range(count)]


def place_first():
    m = np.zeros((32, T1 * 3, 256), np.float32)
    for d in range(T1):
        for r in range(3):
            for a in range(3):
                for b in range(3):
                    for e in range(3):
                        col = (r + b) * 48 + e * 16 + d + a
                        m[9 * a + 3 * b + e, d * 3 + r, col] = 1
    return m.reshape(32, -1)


def place_second():
    m = np.zeros((3, 3, A, 2, 2, 4, 4, A), np.float32)
    c = np.arange(A)
    for d in range(2):
        for r in range(2):
            for a in range(3):
                for b in range(3):
                    m[a, b, c, d, r, d + a, r + b, c] = 1
    return m.reshape(9 * A, 4 * 256)


def place_third():
    m = np.zeros((3, 3, A, 2, R, 4, R, A), np.float32)
    c = np.arange(A)
    for d in range(2):
        for r in range(R):
            for a in range(3):
                for b in range(3):
                    if 0 <= r + b - 1 < R:
                        m[a, b, c, d, r, d + a, r + b - 1, c] = 1
    return m.reshape(9 * A, 2 * R * 256)


def place_halo():
    m = np.zeros((3, A, T1, 16, A), np.float32)
    c = np.arange(A)
    for d in range(T1):
        for a in range(3):
            m[a, c, d, d + a, c] = 1
    return m.reshape(3 * A, T1 * 256)


def place_last(rows, depth):
    n = len(rows)
    m = np.zeros((depth + 2, 3, 8, depth, n, 27), np.float32)
    for d in range(depth):
        for k, r in enumerate(rows):
            for a in range(3):
                for b in range(3):
                    for e in range(3):
                        m[d - (a - 1) + 1, e, r - (b - 1) + 1, d, k, 9 * a + 3 * b + e] = 1
    return m.reshape((depth + 2) * 24, depth * n * 27)


def pick_carried():
    m = np.zeros((4, R, A, A, 4, R), np.float32)
    for d in range(4):
        for r in range(R):
            for o in range(A):
                m[d, r, o, o, d, r] = 1
    return m


def bf(x):
    return jnp.asarray(x, BF)


def dot(a, b):
    return jnp.dot(a, b, preferred_element_type=F32)


def lanes(shape):
    return lax.broadcasted_iota(jnp.int32, shape, len(shape) - 1)


def shifted_sum(low, mid, high):
    lane = lanes(mid.shape)
    low = jnp.where(lane == 0, 0.0, pltpu.roll(low, 1, low.ndim - 1))
    high = jnp.where(lane == W - 1, 0.0, pltpu.roll(high, W - 1, high.ndim - 1))
    return mid + low + high


def combine(p):
    return shifted_sum(p[0:A], p[A : 2 * A], p[2 * A : 3 * A])


def parity():
    return lax.rem(lax.axis_index("rows"), 2)


def edges_kernel(carried, pick, even, odd):
    even_side = 1 - parity()
    pe = pick[even_side]
    po = pick[1 - even_side]
    both = jnp.concatenate([pe, po], axis=0)

    def step(q, _):
        c = carried[:, pl.ds(q * 16, 16), :].reshape(256, W)
        v = dot(both, c).astype(BF)
        even[pl.ds(4 * q, 4)] = v[:64].reshape(4, A, W)
        odd[pl.ds(4 * q, 4)] = v[64:].reshape(4, A, W)
        return 0

    lax.fori_loop(0, carried.shape[1] // 16, step, 0, unroll=4)


def prep_kernel(w1, w2, w3, w4, p1, p2, p3, ph, im, ie, tile, rep, bd, a1, a2, a3, ah, am, ae):
    v = dot(w1[...], p1[...]).astype(BF)
    for k in range(3 * T1):
        a1[pl.ds(k * A, A), :] = v[:, k * 256 : (k + 1) * 256]
    v = dot(w2[...], p2[...]).astype(BF)
    for k in range(4):
        a2[pl.ds(k * 48, 48), :] = v[:, k * 256 : (k + 1) * 256]
    v = dot(w3[...], p3[...]).astype(BF)
    for k in range(2 * R):
        a3[pl.ds(k * 48, 48), :] = v[:, k * 256 : (k + 1) * 256]
    for side in range(2):
        v = dot(ah_source(w3, side), ph[...]).astype(BF)
        for k in range(T1):
            ah[side, pl.ds(k * 48, 48), :] = v[:, k * 256 : (k + 1) * 256]
    t = dot(w4[...], tile[...]).astype(BF)
    blocks = dot(rep[...], t).astype(BF) * bd[...]
    am[...] = dot(im[...], blocks).astype(BF)
    for side in range(2):
        ae[side] = dot(ie[side], blocks).astype(BF)


def ah_source(w3, side):
    b = 2 * side
    v = w3[...]
    return jnp.concatenate([v[:, (3 * a + b) * A : (3 * a + b + 1) * A] for a in range(3)], axis=1)


def corr_kernel(own, mate, partner, pattern, valid, corr, even, odd):
    cam = lax.axis_index("cam")
    right = partner[cam] < cam
    disp = corr.shape[1]
    channels = own.shape[0] // R
    x, y = own[...], mate[...]
    left_side = jnp.where(right, x, y)
    right_side = jnp.where(right, y, x)
    lane = lanes((W, W))
    sub = lax.broadcasted_iota(jnp.int32, (W, W), 0)
    flip = jnp.where(lane + sub == W - 1, 1.0, 0.0).astype(BF)
    lt = dot(left_side, flip).astype(BF).T
    row = lax.rem(lax.broadcasted_iota(jnp.int32, right_side.shape, 0), R)
    zero = jnp.zeros((), BF)
    rs = jnp.concatenate([jnp.where(row == r, right_side, zero) for r in range(R)], axis=1)
    s = dot(lt, rs)
    scale = 1.0 / np.sqrt(channels).astype(np.float32)
    line = lanes((1, W)) // BLOCK_COLS
    for r in range(R):
        v = pltpu.roll(s[:, r * W : (r + 1) * W], 1, 1, stride=1, stride_axis=0)
        v = jnp.where(lane <= sub, v, 0.0).T[:disp] * scale
        v = jnp.concatenate(
            [v[t * DTILE : (t + 1) * DTILE] * pattern[r, t].astype(F32) for t in range(disp // DTILE)], axis=0
        )
        v = dot(v.astype(BF), flip)
        v = jnp.where(right, v, pltpu.roll(v, 0, 1, stride=1, stride_axis=0))
        pixels = jnp.zeros((1, W), F32)
        for k in range(W // BLOCK_COLS):
            pixels = jnp.where(line == k, valid[r, k].astype(F32), pixels)
        corr[r] = (v * pixels).astype(BF)
    side = 1 - parity()
    even[...] = corr[pl.ds(side, 3)]
    odd[...] = corr[pl.ds(1 - side, 3)]


def volume_kernel(
    corr, even, odd, carried, a1, a2, a3, am, pick,
    pre2, pre3, acc,
    ext, cs, h1, h2, h3,
):
    disp = corr.shape[1]
    bands = lax.axis_size("rows")
    me = lax.axis_index("rows")
    side = 1 - parity()
    top_live = (me > 0).astype(F32)
    bottom_live = (me < bands - 1).astype(F32)

    ext[:, 0:8, :] = jnp.zeros((10, 8, W), F32)
    ext[:, pl.ds(8 + disp, 8), :] = jnp.zeros((10, 8, W), F32)
    ext[3:7, pl.ds(8, disp), :] = corr[...].astype(F32)
    ext[pl.ds(7 * side, 3), pl.ds(8, disp), :] = even[...].astype(F32)
    ext[pl.ds(7 * (1 - side), 3), pl.ds(8, disp), :] = odd[...].astype(F32)
    starts = window_starts(disp)
    lane = lanes((16, W))
    for k, d0 in enumerate(starts):
        cs[k, 480:512, :] = jnp.zeros((32, W), BF)
        for r in range(10):
            v = ext[r, d0 + 7 : d0 + 23, :]
            low = jnp.where(lane == 0, 0.0, pltpu.roll(v, 1, 1))
            high = jnp.where(lane == W - 1, 0.0, pltpu.roll(v, W - 1, 1))
            cs[k, r * 48 : r * 48 + 16, :] = low.astype(BF)
            cs[k, r * 48 + 16 : r * 48 + 32, :] = v.astype(BF)
            cs[k, r * 48 + 32 : r * 48 + 48, :] = high.astype(BF)

    zero_row = jnp.zeros((8, A, W), BF)
    h1[0] = zero_row
    h1[disp + 1] = zero_row
    h2[0] = zero_row[:R]
    h2[disp + 1] = zero_row[:R]

    w1 = a1[...]
    for k, d0 in enumerate(starts):
        x = jnp.concatenate([cs[k, pl.ds(j * 48, 256), :] for j in (0, 3, 5)], axis=1)
        p = jnp.maximum(dot(w1, x), 0.0)
        for g, j0 in enumerate((0, 3, 5)):
            q = p[:, g * W : (g + 1) * W].reshape(T1, 3, A, W)
            for t in range(3):
                j = j0 + t
                if g == 2 and t == 0:
                    continue
                v = q[:, t]
                if j < 2:
                    v = v * top_live
                if j > 5:
                    v = v * bottom_live
                h1[pl.ds(1 + d0, T1), j] = v.astype(BF)

    w2 = a2[...]
    sel = pick[...]

    def second(i, _):
        c = carried[:, pl.ds(i * 16, 16), :].reshape(256, W)
        own = dot(sel, c)
        for g in range(3):
            x = jnp.concatenate(
                [h1[pl.ds(4 * i + 2 * h, 4), 2 * g : 2 * g + 4].reshape(256, W) for h in range(2)], axis=1
            )
            p = dot(w2, x)
            for h in range(2):
                for d in range(2):
                    for r in range(2):
                        n = (d * 2 + r) * 48
                        v = combine(p[n : n + 48, h * W : (h + 1) * W])
                        j = 2 * g + r
                        dd = 2 * h + d
                        if j == 0:
                            pre2[0, 4 * i + dd] = v
                        elif j == 5:
                            pre2[1, 4 * i + dd] = v
                        else:
                            m = (dd * R + j - 1) * A
                            v = jnp.maximum(v + own[m : m + A], 0.0)
                            h2[4 * i + dd + 1, j - 1] = v.astype(BF)
        return 0

    lax.fori_loop(0, disp // 4, second, 0)

    w3 = a3[...]

    def third(i, _):
        x = jnp.concatenate([h2[pl.ds(4 * i + 2 * h, 4)].reshape(256, W) for h in range(2)], axis=1)
        p = dot(w3, x)
        for h in range(2):
            for d in range(2):
                for r in range(R):
                    n = (d * R + r) * 48
                    v = combine(p[n : n + 48, h * W : (h + 1) * W])
                    dd = 4 * i + 2 * h + d
                    if r == 0:
                        pre3[0, dd] = v
                    elif r == R - 1:
                        pre3[1, dd] = v
                    else:
                        h3[dd, r - 1] = jnp.maximum(v, 0.0).astype(BF)
        return 0

    lax.fori_loop(0, disp // 4, third, 0)

    acc[0:2] = jnp.zeros((2, 24, W), F32)
    w4 = am[...]
    for k in range(disp // 8):
        p = dot(w4, h3[8 * k : 8 * k + 8].reshape(256, W)).reshape(10, 24, W)
        acc[8 * k : 8 * k + 2] += p[:2]
        acc[8 * k + 2 : 8 * k + 10] = p[2:]


def edge_kernel(
    even, odd, corr, pre2, pre3, acc_in, ah, ae,
    main, part_even, part_odd,
    acc, h2, h3, comb,
):
    disp = corr.shape[1]
    bands = lax.axis_size("rows")
    me = lax.axis_index("rows")
    acc[...] = acc_in[...]
    zero_row = jnp.zeros((A, W), BF)
    starts = window_starts(disp)
    for kind, carried in enumerate((even, odd)):
        side = (1 - parity()) if kind == 0 else parity()
        live = jnp.where(side == 0, me > 0, me < bands - 1).astype(F32)
        h2[0] = zero_row
        h2[disp + 1] = zero_row
        v = jnp.maximum(pre2[side] + carried[...].astype(F32), 0.0) * live
        h2[1 : disp + 1] = v.astype(BF)
        w3 = ah[side]
        for d0 in starts:
            p = dot(w3, h2[d0 : d0 + 16].reshape(256, W))
            for d in range(T1):
                v = combine(p[d * 48 : d * 48 + 48]) + pre3[side, d0 + d]
                h3[d0 + d] = jnp.maximum(v, 0.0).astype(BF)
        w4 = ae[side]
        for k in range(disp // 16):
            p = dot(w4, h3[16 * k : 16 * k + 16].reshape(256, W)).reshape(18, 24, W)
            acc[16 * k : 16 * k + 18] += p

    for d in range(disp):
        comb[d * 8 : d * 8 + 8, :] = shifted_sum(acc[d + 1, 0:8], acc[d + 1, 8:16], acc[d + 1, 16:24])
    side = 1 - parity()
    for r in range(R):
        v = comb[pl.ds(r + 1, disp, stride=8), :] + corr[r].astype(F32)
        main[pl.ds(r, disp, stride=R), :] = v
    top = comb[pl.ds(0, disp, stride=8), :]
    bottom = comb[pl.ds(5, disp, stride=8), :]
    part_even[...] = jnp.where(side == 0, top, bottom)
    part_odd[...] = jnp.where(side == 0, bottom, top)


def call(kernel, outs, args, specs=None, scratch=(), us=2.0):
    return pl.pallas_call(
        kernel,
        out_shape=tuple(jax.ShapeDtypeStruct(s, d) for s, d in outs),
        in_specs=specs or [VM] * len(args),
        out_specs=tuple(VM for _ in outs),
        scratch_shapes=[pltpu.VMEM(s, d) for s, d in scratch],
        compiler_params=pltpu.CompilerParams(vmem_limit_bytes=40 * MIB),
        cost_estimate=pl.CostEstimate(flops=int(us * 1.1e9), bytes_accessed=1000, transcendentals=0),
    )(*args)


def local(features, partner, pattern, valid, carried, w_first, w_second, w_third, w_last):
    channels = features.shape[1]
    disp = carried.shape[2]
    bands = lax.axis_size("rows")
    cams = lax.axis_size("cam")
    even_pairs = [p for k in range(0, bands - 1, 2) for p in ((k, k + 1), (k + 1, k))]
    odd_pairs = [p for k in range(1, bands - 1, 2) for p in ((k, k + 1), (k + 1, k))]

    def swap(x, pairs):
        return lax.ppermute(x, "rows", pairs)

    own = features.reshape(channels * R, W)
    mate = lax.ppermute(own, "cam", [(i, i ^ 1) for i in range(cams)])
    flat = carried.reshape(A, disp * R, W)
    pick = pick_carried()
    ends = np.stack([pick[:, 0], pick[:, R - 1]]).reshape(2, 4 * A, 256)
    edge = ((disp, A, W), BF)
    even_c, odd_c = call(edges_kernel, [edge, edge], [flat, bf(ends)], us=1.5)
    even_c = swap(even_c, even_pairs)
    odd_c = swap(odd_c, odd_pairs)

    w1 = jnp.pad(w_first.T, ((0, 0), (0, 5)))
    rows_of = lambda w: w.reshape(3, 3, 3, A, A).transpose(2, 3, 0, 1, 4).reshape(48, 9 * A)
    w4 = jnp.pad(w_last, ((0, 5), (0, 0)))
    tile = np.tile(np.eye(A), (1, 16))
    rep = np.pad(np.tile(np.eye(27), (16, 1)), ((0, 0), (0, 5)))
    mask = np.kron(np.eye(16), np.ones((27, A)))
    ie = np.stack([place_last([0], 16), place_last([R - 1], 16)])
    consts = [place_first(), place_second(), place_third(), place_halo(), place_last([1, 2], 8), ie, tile, rep, mask]
    mats = [
        ((T1 * 48, 256), BF),
        ((192, 256), BF),
        ((384, 256), BF),
        ((2, T1 * 48, 256), BF),
        ((240, 256), BF),
        ((2, 432, 256), BF),
    ]
    a1, a2, a3, ah, am, ae = call(
        prep_kernel, mats, [w1, rows_of(w_second), rows_of(w_third), w4] + [bf(c) for c in consts], us=1.5
    )

    rows3 = ((3, disp, W), BF)
    corr, even_r, odd_r = call(
        corr_kernel,
        [((R, disp, W), BF), rows3, rows3],
        [own, mate, partner, pattern, valid[0]],
        specs=[VM, VM, SM, SM, SM],
        us=2.0,
    )
    even_r = swap(even_r, even_pairs)
    odd_r = swap(odd_r, odd_pairs)
    pre = ((2, disp, A, W), F32)
    pre2, pre3, acc = call(
        volume_kernel,
        [pre, pre, ((disp + 2, 24, W), F32)],
        [corr, even_r, odd_r, flat, a1, a2, a3, am, bf(pick.reshape(256, 256))],
        scratch=[
            ((10, disp + 16, W), F32),
            ((len(window_starts(disp)), 512, W), BF),
            ((disp + 2, 8, A, W), BF),
            ((disp + 2, R, A, W), BF),
            ((disp, 2, A, W), BF),
        ],
        us=10.0,
    )
    main, part_even, part_odd = call(
        edge_kernel,
        [((disp * R, W), F32), ((disp, W), F32), ((disp, W), F32)],
        [even_c, odd_c, corr, pre2, pre3, acc, ah, ae],
        scratch=[
            ((disp + 2, 24, W), F32),
            ((disp + 2, A, W), BF),
            ((disp, A, W), BF),
            ((disp * 8, W), F32),
        ],
        us=4.0,
    )
    part_even = swap(part_even, even_pairs)
    part_odd = swap(part_odd, odd_pairs)
    is_odd = lax.rem(lax.axis_index("rows"), 2) == 1
    top = jnp.where(is_odd, part_even, part_odd)[:, None]
    bottom = jnp.where(is_odd, part_odd, part_even)[:, None]
    none = jnp.zeros((disp, R - 2, W), F32)
    out = main.reshape(disp, R, W) + jnp.concatenate([top, none, bottom], axis=1)
    return out[None]


def solution(mesh):
    return jax.shard_map(
        local,
        mesh=mesh,
        in_specs=(
            P(("seg", "cam"), None, "rows", None),
            P(),
            P(("seg", "rows"), None),
            P(("seg", "cam"), "rows", None),
            P(("seg", "cam"), None, None, "rows", None),
            P(),
            P(),
            P(),
            P(),
        ),
        out_specs=P(("seg", "cam"), None, "rows", None),
        check_vma=False,
    )
```

```python
import numpy as np
import jax
import jax.numpy as jnp
from jax import lax
from jax.experimental import pallas as pl
from jax.experimental.pallas import tpu as pltpu
from jax.sharding import PartitionSpec as P

DTILE = 16
BLOCK_COLS = 32
BF = jnp.bfloat16
F32 = jnp.float32
VM = pl.BlockSpec(memory_space=pltpu.VMEM)
SM = pl.BlockSpec(memory_space=pltpu.SMEM)
HB = pl.BlockSpec(memory_space=pltpu.HBM)
MIB = 2**20

R, W, A = 4, 128, 16
T1 = 14


def window_starts(disp):
    count = -(-disp // T1)
    return [min(T1 * k, disp - T1) for k in range(count)]


def place_first():
    m = np.zeros((27, T1 * 3, 256), np.float32)
    for d in range(T1):
        for r in range(3):
            for a in range(3):
                for b in range(3):
                    for e in range(3):
                        col = (r + b) * 48 + e * 16 + d + a
                        m[9 * a + 3 * b + e, d * 3 + r, col] = 1
    return m.reshape(27, -1)


def place_second():
    m = np.zeros((3, 3, A, 2, 2, 4, 4, A), np.float32)
    c = np.arange(A)
    for d in range(2):
        for r in range(2):
            for a in range(3):
                for b in range(3):
                    m[a, b, c, d, r, d + a, r + b, c] = 1
    return m.reshape(9 * A, 4 * 256)


def place_third():
    m = np.zeros((3, 3, A, 2, R, 4, R, A), np.float32)
    c = np.arange(A)
    for d in range(2):
        for r in range(R):
            for a in range(3):
                for b in range(3):
                    if 0 <= r + b - 1 < R:
                        m[a, b, c, d, r, d + a, r + b - 1, c] = 1
    return m.reshape(9 * A, 2 * R * 256)


def place_halo():
    m = np.zeros((3, A, T1, 16, A), np.float32)
    c = np.arange(A)
    for d in range(T1):
        for a in range(3):
            m[a, c, d, d + a, c] = 1
    return m.reshape(3 * A, T1 * 256)


def place_last(rows, depth):
    n = len(rows)
    m = np.zeros((depth + 2, 3, 8, depth, n, 27), np.float32)
    for d in range(depth):
        for k, r in enumerate(rows):
            for a in range(3):
                for b in range(3):
                    for e in range(3):
                        m[d - (a - 1) + 1, e, r - (b - 1) + 1, d, k, 9 * a + 3 * b + e] = 1
    return m.reshape((depth + 2) * 24, depth * n * 27)


def pick_carried():
    m = np.zeros((4, R, A, A, 4, R), np.float32)
    for d in range(4):
        for r in range(R):
            for o in range(A):
                m[d, r, o, o, d, r] = 1
    return m


def bf(x):
    return jnp.asarray(x, BF)


def dot(a, b):
    return jnp.dot(a, b, preferred_element_type=F32)


def lanes(shape):
    return lax.broadcasted_iota(jnp.int32, shape, len(shape) - 1)


def shifted_sum(low, mid, high):
    lane = lanes(mid.shape)
    low = jnp.where(lane == 0, 0.0, pltpu.roll(low, 1, low.ndim - 1))
    high = jnp.where(lane == W - 1, 0.0, pltpu.roll(high, W - 1, high.ndim - 1))
    return mid + low + high


def combine(p):
    return shifted_sum(p[0:A], p[A : 2 * A], p[2 * A : 3 * A])


def parity():
    return lax.rem(lax.axis_index("rows"), 2)


def edge_pick(row):
    m = lax.broadcasted_iota(jnp.int32, (4 * A, 256), 0)
    n = lax.broadcasted_iota(jnp.int32, (4 * A, 256), 1)
    want = (m % A) * 16 + (m // A) * R + row
    return jnp.where(n == want, 1.0, 0.0).astype(BF)


def edges_kernel(
    carried, features, partner, pattern, valid,
    even, odd, own, masks, right,
    buf, sems, partner_s, pattern_s, valid_s, own_sem, small_sems,
):
    parts = sems.shape[0]
    size = carried.shape[1] // parts
    copies = []
    for k in range(parts):
        at = pl.ds(k * size, size)
        copies.append(pltpu.make_async_copy(carried.at[:, at, :], buf.at[:, at, :], sems.at[k]))
        copies[-1].start()
    load_own = pltpu.make_async_copy(features, own, own_sem)
    load_own.start()
    small = [
        pltpu.make_async_copy(a, b, small_sems.at[k])
        for k, (a, b) in enumerate(((partner, partner_s), (pattern, pattern_s), (valid, valid_s)))
    ]
    for c in small:
        c.start()
    last = R - 1
    even_row = jnp.where(parity() == 0, last, 0)
    both = jnp.concatenate([edge_pick(even_row), edge_pick(last - even_row)], axis=0)
    for q in range(carried.shape[1] // 16):
        if q % (size // 16) == 0:
            copies[q // (size // 16)].wait()
        v = dot(both, buf[:, q * 16 : q * 16 + 16, :].reshape(256, W)).astype(BF)
        even[4 * q : 4 * q + 4] = v[:64].reshape(4, A, W)
        odd[4 * q : 4 * q + 4] = v[64:].reshape(4, A, W)
    for c in small:
        c.wait()
    cam = lax.axis_index("cam")
    flag = jnp.where(partner_s[cam] < cam, 1.0, 0.0)
    right[...] = jnp.full((8, W), flag, F32)
    line = lanes((DTILE, W)) // BLOCK_COLS
    for r in range(R):
        pixels = jnp.zeros((DTILE, W), F32)
        for k in range(W // BLOCK_COLS):
            pixels = jnp.where(line == k, valid_s[0, r, k].astype(F32), pixels)
        for t in range(masks.shape[1] // DTILE):
            masks[r, t * DTILE : (t + 1) * DTILE, :] = pixels * pattern_s[r, t].astype(F32)
    load_own.wait()


def ordered(w):
    outs = []
    v = w[...]
    for e in range(3):
        t = lax.broadcasted_iota(jnp.int32, (27, 9 * A), 0)
        n = lax.broadcasted_iota(jnp.int32, (27, 9 * A), 1)
        take = jnp.where(t == (n // A) * 3 + e, 1.0, 0.0).astype(BF)
        spread = dot(v, take)
        m = lax.broadcasted_iota(jnp.int32, spread.shape, 0)
        n = lax.broadcasted_iota(jnp.int32, spread.shape, 1)
        spread = jnp.where(m % A == n % A, spread, 0.0).astype(BF)
        o = lax.broadcasted_iota(jnp.int32, (A, A * A), 0)
        m = lax.broadcasted_iota(jnp.int32, (A, A * A), 1)
        gather = jnp.where(m // A == o, 1.0, 0.0).astype(BF)
        outs.append(dot(gather, spread).astype(BF))
    return jnp.concatenate(outs, axis=0)


def place_weights(w1, w2, w3, w4, p1, p2, p3, ph, im, ie, a1, a2, a3, ah, am, ae):
    v = dot(w1[...], p1[...]).astype(BF)
    for k in range(3 * T1):
        a1[pl.ds(k * A, A), :] = v[:, k * 256 : (k + 1) * 256]
    v = dot(ordered(w2), p2[...]).astype(BF)
    for k in range(4):
        a2[pl.ds(k * 48, 48), :] = v[:, k * 256 : (k + 1) * 256]
    third = ordered(w3)
    v = dot(third, p3[...]).astype(BF)
    for k in range(2 * R):
        a3[pl.ds(k * 48, 48), :] = v[:, k * 256 : (k + 1) * 256]
    for side in range(2):
        v = dot(ah_source(third, side), ph[...]).astype(BF)
        for k in range(T1):
            ah[side, pl.ds(k * 48, 48), :] = v[:, k * 256 : (k + 1) * 256]
    m = lax.broadcasted_iota(jnp.int32, (432, 27), 0)
    n = lax.broadcasted_iota(jnp.int32, (432, 27), 1)
    tall = jnp.where(m % 27 == n, 1.0, 0.0).astype(BF)
    tall = lax.dot_general(tall, w4[...], (((1,), (1,)), ((), ())), preferred_element_type=F32).astype(BF)
    m = lax.broadcasted_iota(jnp.int32, (A, 256), 0)
    n = lax.broadcasted_iota(jnp.int32, (A, 256), 1)
    wide = jnp.where(n % A == m, 1.0, 0.0).astype(BF)
    blocks = dot(tall, wide)
    m = lax.broadcasted_iota(jnp.int32, (432, 256), 0)
    n = lax.broadcasted_iota(jnp.int32, (432, 256), 1)
    blocks = jnp.where(m // 27 == n // A, blocks, 0.0).astype(BF)
    am[...] = dot(im[...], blocks).astype(BF)
    for side in range(2):
        ae[side] = dot(ie[side], blocks).astype(BF)


def ah_source(w3, side):
    b = 2 * side
    return jnp.concatenate([w3[:, (3 * a + b) * A : (3 * a + b + 1) * A] for a in range(3)], axis=1)


def corr_kernel(own, mate, masks, right_ref, even_c, odd_c, corr, even, odd, even_out, odd_out):
    right = right_ref[0:1, :] > 0.5
    disp = corr.shape[1]
    channels = own.shape[0] // R
    x, y = own[...], mate[...]
    left_side = jnp.where(right, x, y)
    right_side = jnp.where(right, y, x)
    lane = lanes((W, W))
    sub = lax.broadcasted_iota(jnp.int32, (W, W), 0)
    flip = jnp.where(lane + sub == W - 1, 1.0, 0.0).astype(BF)
    lt = dot(left_side, flip).astype(BF).T
    row = lax.rem(lax.broadcasted_iota(jnp.int32, right_side.shape, 0), R)
    zero = jnp.zeros((), BF)
    rs = jnp.concatenate([jnp.where(row == r, right_side, zero) for r in range(R)], axis=1)
    s = dot(lt, rs)
    scale = 1.0 / np.sqrt(channels).astype(np.float32)
    for r in range(R):
        v = pltpu.roll(s[:, r * W : (r + 1) * W], 1, 1, stride=1, stride_axis=0)
        v = jnp.where(lane <= sub, v, 0.0).T[:disp] * scale
        v = dot(v.astype(BF), flip)
        v = jnp.where(right, v, pltpu.roll(v, 0, 1, stride=1, stride_axis=0))
        corr[r] = (v * masks[r]).astype(BF)
    side = 1 - parity()
    even[...] = corr[pl.ds(side, 3)]
    odd[...] = corr[pl.ds(1 - side, 3)]
    even_out[...] = even_c[...]
    odd_out[...] = odd_c[...]


def volume_kernel(
    corr, even, odd, carried_hbm, pick_hbm,
    w1_hbm, w2_hbm, w3_hbm, w4_hbm, p1_hbm, p2_hbm, p3_hbm, ph_hbm, im_hbm, ie_hbm,
    pre2, pre3, main, ah, ae,
    ext, cs, h1, h2, h3, acc, comb, a1, a2, a3, am,
    carried, pick, w1, w2, w3, w4, p1, p2, p3, ph, im, ie, sems,
):
    far = (w1_hbm, w2_hbm, w3_hbm, w4_hbm, p1_hbm, p2_hbm, p3_hbm, ph_hbm, im_hbm, ie_hbm, pick_hbm, carried_hbm)
    near = (w1, w2, w3, w4, p1, p2, p3, ph, im, ie, pick, carried)
    copies = [pltpu.make_async_copy(a, b, sems.at[k]) for k, (a, b) in enumerate(zip(far, near))]
    for c in copies:
        c.start()
    for c in copies[:10]:
        c.wait()
    place_weights(w1, w2, w3, w4, p1, p2, p3, ph, im, ie, a1, a2, a3, ah, am, ae)
    for c in copies[10:]:
        c.wait()
    disp = corr.shape[1]
    bands = lax.axis_size("rows")
    me = lax.axis_index("rows")
    side = 1 - parity()
    top_live = (me > 0).astype(F32)
    bottom_live = (me < bands - 1).astype(F32)

    ext[:, 0:8, :] = jnp.zeros((10, 8, W), F32)
    ext[:, pl.ds(8 + disp, 8), :] = jnp.zeros((10, 8, W), F32)
    ext[3:7, pl.ds(8, disp), :] = corr[...].astype(F32)
    ext[pl.ds(7 * side, 3), pl.ds(8, disp), :] = even[...].astype(F32)
    ext[pl.ds(7 * (1 - side), 3), pl.ds(8, disp), :] = odd[...].astype(F32)
    starts = window_starts(disp)
    lane = lanes((16, W))
    for k, d0 in enumerate(starts):
        cs[k, 480:512, :] = jnp.zeros((32, W), BF)
        for r in range(10):
            v = ext[r, d0 + 7 : d0 + 23, :]
            low = jnp.where(lane == 0, 0.0, pltpu.roll(v, 1, 1))
            high = jnp.where(lane == W - 1, 0.0, pltpu.roll(v, W - 1, 1))
            cs[k, r * 48 : r * 48 + 16, :] = low.astype(BF)
            cs[k, r * 48 + 16 : r * 48 + 32, :] = v.astype(BF)
            cs[k, r * 48 + 32 : r * 48 + 48, :] = high.astype(BF)

    zero_row = jnp.zeros((8, A, W), BF)
    h1[0] = zero_row
    h1[disp + 1] = zero_row
    h2[0] = zero_row[:R]
    h2[disp + 1] = zero_row[:R]

    w1 = a1[...]
    for k, d0 in enumerate(starts):
        x = jnp.concatenate([cs[k, pl.ds(j * 48, 256), :] for j in (0, 3, 5)], axis=1)
        p = jnp.maximum(dot(w1, x), 0.0)
        for g, j0 in enumerate((0, 3, 5)):
            q = p[:, g * W : (g + 1) * W].reshape(T1, 3, A, W)
            for t in range(3):
                j = j0 + t
                if g == 2 and t == 0:
                    continue
                v = q[:, t]
                if j < 2:
                    v = v * top_live
                if j > 5:
                    v = v * bottom_live
                h1[pl.ds(1 + d0, T1), j] = v.astype(BF)

    w2 = a2[...]
    sel = pick[...]

    for i in range(disp // 4):
        c = carried[:, pl.ds(i * 16, 16), :].reshape(256, W)
        own = dot(sel, c)
        for g in range(3):
            x = jnp.concatenate(
                [h1[pl.ds(4 * i + 2 * h, 4), 2 * g : 2 * g + 4].reshape(256, W) for h in range(2)], axis=1
            )
            p = dot(w2, x)
            for h in range(2):
                for d in range(2):
                    for r in range(2):
                        n = (d * 2 + r) * 48
                        v = combine(p[n : n + 48, h * W : (h + 1) * W])
                        j = 2 * g + r
                        dd = 2 * h + d
                        if j == 0:
                            pre2[0, 4 * i + dd] = v
                        elif j == 5:
                            pre2[1, 4 * i + dd] = v
                        else:
                            m = (dd * R + j - 1) * A
                            v = jnp.maximum(v + own[m : m + A], 0.0)
                            h2[4 * i + dd + 1, j - 1] = v.astype(BF)

    w3 = a3[...]

    for i in range(disp // 4):
        x = jnp.concatenate([h2[pl.ds(4 * i + 2 * h, 4)].reshape(256, W) for h in range(2)], axis=1)
        p = dot(w3, x)
        for h in range(2):
            for d in range(2):
                for r in range(R):
                    n = (d * R + r) * 48
                    v = combine(p[n : n + 48, h * W : (h + 1) * W])
                    dd = 4 * i + 2 * h + d
                    if r == 0:
                        pre3[0, dd] = v
                    elif r == R - 1:
                        pre3[1, dd] = v
                    else:
                        h3[dd, r - 1] = jnp.maximum(v, 0.0).astype(BF)

    acc[0:2] = jnp.zeros((2, 24, W), F32)
    w4 = am[...]
    for k in range(disp // 8):
        p = dot(w4, h3[8 * k : 8 * k + 8].reshape(256, W)).reshape(10, 24, W)
        acc[8 * k : 8 * k + 2] += p[:2]
        acc[8 * k + 2 : 8 * k + 10] = p[2:]
    sum_columns(acc, comb, disp)
    for r in range(R):
        main[r] = comb[pl.ds(r + 1, disp, stride=8), :] + corr[r].astype(F32)


def sum_columns(acc, comb, disp):
    for d in range(disp):
        comb[d * 8 : d * 8 + 8, :] = shifted_sum(acc[d + 1, 0:8], acc[d + 1, 8:16], acc[d + 1, 16:24])


def edge_rows(side, carried, pre2, pre3, ah, ae, acc, h2, h3, comb):
    disp = carried.shape[0]
    me = lax.axis_index("rows")
    live = jnp.where(side == 0, me > 0, me < lax.axis_size("rows") - 1).astype(F32)
    zero_row = jnp.zeros((A, W), BF)
    h2[0] = zero_row
    h2[disp + 1] = zero_row
    v = jnp.maximum(pre2[...] + carried[...].astype(F32), 0.0) * live
    h2[1 : disp + 1] = v.astype(BF)
    w3 = ah[side]
    for d0 in window_starts(disp):
        p = dot(w3, h2[d0 : d0 + 16].reshape(256, W))
        for d in range(T1):
            v = combine(p[d * 48 : d * 48 + 48]) + pre3[d0 + d]
            h3[d0 + d] = jnp.maximum(v, 0.0).astype(BF)
    w4 = ae[side]
    acc[0:2] = jnp.zeros((2, 24, W), F32)
    for k in range(disp // 16):
        p = dot(w4, h3[16 * k : 16 * k + 16].reshape(256, W)).reshape(18, 24, W)
        acc[16 * k : 16 * k + 2] += p[:2]
        acc[16 * k + 2 : 16 * k + 18] = p[2:]
    sum_columns(acc, comb, disp)


def first_kernel(carried, main_in, pre2, pre3, ah, ae, main, part, pre2_rest, pre3_rest, acc, h2, h3, comb):
    disp = carried.shape[0]
    side = parity()
    edge_rows(side, carried, pre2.at[side], pre3.at[side], ah, ae, acc, h2, h3, comb)
    main[...] = main_in[...]
    for k in range(2):
        main[2 * side + k] += comb[pl.ds(2 * side + 1 + k, disp, stride=8), :]
    part[...] = comb[pl.ds(5 * side, disp, stride=8), :]
    pre2_rest[...] = pre2[1 - side]
    pre3_rest[...] = pre3[1 - side]


def last_kernel(carried, main_in, received, pre2, pre3, ah, ae, main, part, acc, h2, h3, comb):
    disp = carried.shape[0]
    side = 1 - parity()
    edge_rows(side, carried, pre2, pre3, ah, ae, acc, h2, h3, comb)
    for r in range(R):
        v = main_in[r] + jnp.where(side == r // 2, comb[pl.ds(r + 1, disp, stride=8), :], 0.0)
        if r in (0, R - 1):
            v += jnp.where(side == r // 2, 0.0, received[...])
        main[pl.ds(r, disp, stride=R), :] = v
    part[...] = comb[pl.ds(5 * side, disp, stride=8), :]


def add_kernel(main, part, out):
    disp = part.shape[0]
    out[...] = main[...]
    odd_band = parity() == 1
    for r in (0, R - 1):
        at = pl.ds(r, disp, stride=R)
        mine = odd_band if r == 0 else jnp.logical_not(odd_band)
        out[at, :] += jnp.where(mine, part[...], 0.0)


def call(kernel, outs, args, specs=None, scratch=(), sems=0, us=2.0):
    return pl.pallas_call(
        kernel,
        out_shape=tuple(jax.ShapeDtypeStruct(s, d) for s, d in outs),
        in_specs=specs or [VM] * len(args),
        out_specs=tuple(VM for _ in outs),
        scratch_shapes=[pltpu.VMEM(s, d) for s, d in scratch] + [pltpu.SemaphoreType.DMA((sems,))] * (sems > 0),
        compiler_params=pltpu.CompilerParams(vmem_limit_bytes=24 * MIB),
        cost_estimate=pl.CostEstimate(flops=int(us * 1.1e9), bytes_accessed=1000, transcendentals=0),
    )(*args)


def local(features, partner, pattern, valid, carried, w_first, w_second, w_third, w_last):
    channels = features.shape[1]
    disp = carried.shape[2]
    bands = lax.axis_size("rows")
    cams = lax.axis_size("cam")
    even_pairs = [p for k in range(0, bands - 1, 2) for p in ((k, k + 1), (k + 1, k))]
    odd_pairs = [p for k in range(1, bands - 1, 2) for p in ((k, k + 1), (k + 1, k))]

    def swap(x, pairs):
        return lax.ppermute(x, "rows", pairs)

    own = features.reshape(channels * R, W)
    mate = lax.ppermute(own, "cam", [(i, i ^ 1) for i in range(cams)])
    flat = carried.reshape(A, disp * R, W)
    edge = ((disp, A, W), BF)
    parts = 4
    even_c, odd_c, own, masks, right = pl.pallas_call(
        edges_kernel,
        out_shape=tuple(
            jax.ShapeDtypeStruct(s, d)
            for s, d in (edge, edge, (own.shape, BF), ((R, disp, W), F32), ((8, W), F32))
        ),
        in_specs=[HB] * 5,
        out_specs=(VM,) * 5,
        scratch_shapes=[
            pltpu.VMEM(flat.shape, BF),
            pltpu.SemaphoreType.DMA((parts,)),
            pltpu.SMEM(partner.shape, jnp.int32),
            pltpu.SMEM(pattern.shape, jnp.int32),
            pltpu.SMEM(valid.shape, jnp.int32),
            pltpu.SemaphoreType.DMA,
            pltpu.SemaphoreType.DMA((3,)),
        ],
        compiler_params=pltpu.CompilerParams(vmem_limit_bytes=24 * MIB),
        cost_estimate=pl.CostEstimate(flops=2 * 10**9, bytes_accessed=1000, transcendentals=0),
    )(flat, own, partner, pattern, valid)

    rows3 = ((3, disp, W), BF)
    corr, even_r, odd_r, even_c, odd_c = call(
        corr_kernel,
        [((R, disp, W), BF), rows3, rows3, edge, edge],
        [own, mate, masks, right, even_c, odd_c],
        us=2.0,
    )
    odd_r = swap(odd_r, odd_pairs)
    even_r = swap(even_r, even_pairs)
    odd_c = swap(odd_c, odd_pairs)
    even_c = swap(even_c, even_pairs)

    by_tap = lambda w: w.transpose(1, 2, 0).reshape(A * A, 27)
    ie = np.stack([place_last([0], 16), place_last([R - 1], 16)])
    consts = [place_first(), place_second(), place_third(), place_halo(), place_last([1, 2], 8), ie]
    far = [flat, bf(pick_carried().reshape(256, 256)), w_first.T, by_tap(w_second), by_tap(w_third), w_last.T]
    far += [bf(c) for c in consts]
    pre = ((2, disp, A, W), F32)
    rows = ((R, disp, W), F32)
    line = ((disp, W), F32)
    pre2, pre3, main, ah, ae = call(
        volume_kernel,
        [pre, pre, rows, ((2, T1 * 48, 256), BF), ((2, 432, 256), BF)],
        [corr, even_r, odd_r] + far,
        specs=[VM] * 3 + [HB] * len(far),
        scratch=[
            ((10, disp + 16, W), F32),
            ((len(window_starts(disp)), 512, W), BF),
            ((disp + 2, 8, A, W), BF),
            ((disp + 2, R, A, W), BF),
            ((disp, 2, A, W), BF),
            ((disp + 2, 24, W), F32),
            ((disp * 8, W), F32),
            ((T1 * 48, 256), BF),
            ((192, 256), BF),
            ((384, 256), BF),
            ((240, 256), BF),
        ]
        + [(x.shape, BF) for x in far],
        sems=len(far),
        us=8.0,
    )
    scratch = [
        ((disp + 2, 24, W), F32),
        ((disp + 2, A, W), BF),
        ((disp, A, W), BF),
        ((disp * 8, W), F32),
    ]
    half = ((disp, A, W), F32)
    main, part, pre2, pre3 = call(
        first_kernel, [rows, line, half, half], [odd_c, main, pre2, pre3, ah, ae], scratch=scratch, us=2.0
    )
    part = swap(part, odd_pairs)
    flat_rows = ((disp * R, W), F32)
    main, part = call(
        last_kernel, [flat_rows, line], [even_c, main, part, pre2, pre3, ah, ae], scratch=scratch, us=2.0
    )
    part = swap(part, even_pairs)
    (out,) = call(add_kernel, [flat_rows], [main, part], us=0.3)
    return out.reshape(1, disp, R, W)


def solution(mesh):
    return jax.shard_map(
        local,
        mesh=mesh,
        in_specs=(
            P(("seg", "cam"), None, "rows", None),
            P(),
            P(("seg", "rows"), None),
            P(("seg", "cam"), "rows", None),
            P(("seg", "cam"), None, None, "rows", None),
            P(),
            P(),
            P(),
            P(),
        ),
        out_specs=P(("seg", "cam"), None, "rows", None),
        check_vma=False,
    )
```

```python
import numpy as np
import jax
import jax.numpy as jnp
from jax import lax
from jax.experimental import pallas as pl
from jax.experimental.pallas import tpu as pltpu
from jax.sharding import PartitionSpec as P

DTILE = 16
BLOCK_COLS = 32
BF = jnp.bfloat16
F32 = jnp.float32
VM = pl.BlockSpec(memory_space=pltpu.VMEM)
SM = pl.BlockSpec(memory_space=pltpu.SMEM)
HB = pl.BlockSpec(memory_space=pltpu.HBM)
MIB = 2**20
EDGES, CORR, VOL, EDGE = 1.5, 1.5, 8.0, 2.0

R, W, A = 4, 128, 16
T1 = 14


def window_starts(disp):
    count = -(-disp // T1)
    return [min(T1 * k, disp - T1) for k in range(count)]


def place_first():
    m = np.zeros((27, T1 * 3, 256), np.float32)
    for d in range(T1):
        for r in range(3):
            for a in range(3):
                for b in range(3):
                    for e in range(3):
                        col = (r + b) * 48 + e * 16 + d + a
                        m[9 * a + 3 * b + e, d * 3 + r, col] = 1
    return m.reshape(27, -1)


def place_second():
    m = np.zeros((3, 3, A, 2, 2, 4, 4, A), np.float32)
    c = np.arange(A)
    for d in range(2):
        for r in range(2):
            for a in range(3):
                for b in range(3):
                    m[a, b, c, d, r, d + a, r + b, c] = 1
    return m.reshape(9 * A, 4 * 256)


def place_third():
    m = np.zeros((3, 3, A, 2, R, 4, R, A), np.float32)
    c = np.arange(A)
    for d in range(2):
        for r in range(R):
            for a in range(3):
                for b in range(3):
                    if 0 <= r + b - 1 < R:
                        m[a, b, c, d, r, d + a, r + b - 1, c] = 1
    return m.reshape(9 * A, 2 * R * 256)


def place_halo():
    m = np.zeros((3, A, T1, 16, A), np.float32)
    c = np.arange(A)
    for d in range(T1):
        for a in range(3):
            m[a, c, d, d + a, c] = 1
    return m.reshape(3 * A, T1 * 256)


def place_last(rows, depth):
    n = len(rows)
    m = np.zeros((depth + 2, 3, 8, depth, n, 27), np.float32)
    for d in range(depth):
        for k, r in enumerate(rows):
            for a in range(3):
                for b in range(3):
                    for e in range(3):
                        m[d - (a - 1) + 1, e, r - (b - 1) + 1, d, k, 9 * a + 3 * b + e] = 1
    return m.reshape((depth + 2) * 24, depth * n * 27)


def pick_carried():
    m = np.zeros((4, R, A, A, 4, R), np.float32)
    for d in range(4):
        for r in range(R):
            for o in range(A):
                m[d, r, o, o, d, r] = 1
    return m


def bf(x):
    return jnp.asarray(x, BF)


def dot(a, b):
    return jnp.dot(a, b, preferred_element_type=F32)


def lanes(shape):
    return lax.broadcasted_iota(jnp.int32, shape, len(shape) - 1)


def shifted_sum(low, mid, high):
    lane = lanes(mid.shape)
    low = jnp.where(lane == 0, 0.0, pltpu.roll(low, 1, low.ndim - 1))
    high = jnp.where(lane == W - 1, 0.0, pltpu.roll(high, W - 1, high.ndim - 1))
    return mid + low + high


def combine(p):
    return shifted_sum(p[0:A], p[A : 2 * A], p[2 * A : 3 * A])


def parity():
    return lax.rem(lax.axis_index("rows"), 2)


def edge_pick(row):
    m = lax.broadcasted_iota(jnp.int32, (4 * A, 256), 0)
    n = lax.broadcasted_iota(jnp.int32, (4 * A, 256), 1)
    want = (m % A) * 16 + (m // A) * R + row
    return jnp.where(n == want, 1.0, 0.0).astype(BF)


def edges_kernel(carried, even, odd):
    last = R - 1
    even_row = jnp.where(parity() == 0, last, 0)
    both = jnp.concatenate([edge_pick(even_row), edge_pick(last - even_row)], axis=0)
    for q in range(carried.shape[1] // 16):
        v = dot(both, carried[:, q * 16 : q * 16 + 16, :].reshape(256, W)).astype(BF)
        even[4 * q : 4 * q + 4] = v[:64].reshape(4, A, W)
        odd[4 * q : 4 * q + 4] = v[64:].reshape(4, A, W)


def ordered(w):
    outs = []
    v = w[...]
    for e in range(3):
        t = lax.broadcasted_iota(jnp.int32, (27, 9 * A), 0)
        n = lax.broadcasted_iota(jnp.int32, (27, 9 * A), 1)
        take = jnp.where(t == (n // A) * 3 + e, 1.0, 0.0).astype(BF)
        spread = dot(v, take)
        m = lax.broadcasted_iota(jnp.int32, spread.shape, 0)
        n = lax.broadcasted_iota(jnp.int32, spread.shape, 1)
        spread = jnp.where(m % A == n % A, spread, 0.0).astype(BF)
        o = lax.broadcasted_iota(jnp.int32, (A, A * A), 0)
        m = lax.broadcasted_iota(jnp.int32, (A, A * A), 1)
        gather = jnp.where(m // A == o, 1.0, 0.0).astype(BF)
        outs.append(dot(gather, spread).astype(BF))
    return jnp.concatenate(outs, axis=0)


def place_weights(w1, w2, w3, w4, p1, p2, p3, ph, im, ie, a1, a2, a3, ah, am, ae):
    v = dot(w1[...], p1[...]).astype(BF)
    for k in range(3 * T1):
        a1[pl.ds(k * A, A), :] = v[:, k * 256 : (k + 1) * 256]
    v = dot(ordered(w2), p2[...]).astype(BF)
    for k in range(4):
        a2[pl.ds(k * 48, 48), :] = v[:, k * 256 : (k + 1) * 256]
    third = ordered(w3)
    v = dot(third, p3[...]).astype(BF)
    for k in range(2 * R):
        a3[pl.ds(k * 48, 48), :] = v[:, k * 256 : (k + 1) * 256]
    for side in range(2):
        v = dot(ah_source(third, side), ph[...]).astype(BF)
        for k in range(T1):
            ah[side, pl.ds(k * 48, 48), :] = v[:, k * 256 : (k + 1) * 256]
    m = lax.broadcasted_iota(jnp.int32, (432, 27), 0)
    n = lax.broadcasted_iota(jnp.int32, (432, 27), 1)
    tall = jnp.where(m % 27 == n, 1.0, 0.0).astype(BF)
    tall = lax.dot_general(tall, w4[...], (((1,), (1,)), ((), ())), preferred_element_type=F32).astype(BF)
    m = lax.broadcasted_iota(jnp.int32, (A, 256), 0)
    n = lax.broadcasted_iota(jnp.int32, (A, 256), 1)
    wide = jnp.where(n % A == m, 1.0, 0.0).astype(BF)
    blocks = dot(tall, wide)
    m = lax.broadcasted_iota(jnp.int32, (432, 256), 0)
    n = lax.broadcasted_iota(jnp.int32, (432, 256), 1)
    blocks = jnp.where(m // 27 == n // A, blocks, 0.0).astype(BF)
    am[...] = dot(im[...], blocks).astype(BF)
    for side in range(2):
        ae[side] = dot(ie[side], blocks).astype(BF)


def ah_source(w3, side):
    b = 2 * side
    return jnp.concatenate([w3[:, (3 * a + b) * A : (3 * a + b + 1) * A] for a in range(3)], axis=1)


def corr_kernel(own, mate, partner, pattern, valid, even_c, odd_c, corr, even, odd, even_out, odd_out):
    cam = lax.axis_index("cam")
    right = partner[cam] < cam
    line = lanes((1, W)) // BLOCK_COLS
    disp = corr.shape[1]
    channels = own.shape[0] // R
    x, y = own[...], mate[...]
    left_side = jnp.where(right, x, y)
    right_side = jnp.where(right, y, x)
    lane = lanes((W, W))
    sub = lax.broadcasted_iota(jnp.int32, (W, W), 0)
    flip = jnp.where(lane + sub == W - 1, 1.0, 0.0).astype(BF)
    lt = dot(left_side, flip).astype(BF).T
    row = lax.rem(lax.broadcasted_iota(jnp.int32, right_side.shape, 0), R)
    zero = jnp.zeros((), BF)
    rs = jnp.concatenate([jnp.where(row == r, right_side, zero) for r in range(R)], axis=1)
    s = dot(lt, rs)
    scale = 1.0 / np.sqrt(channels).astype(np.float32)
    for r in range(R):
        v = pltpu.roll(s[:, r * W : (r + 1) * W], 1, 1, stride=1, stride_axis=0)
        v = jnp.where(lane <= sub, v, 0.0).T[:disp] * scale
        v = jnp.concatenate(
            [v[t * DTILE : (t + 1) * DTILE] * pattern[r, t].astype(F32) for t in range(disp // DTILE)], axis=0
        )
        v = dot(v.astype(BF), flip)
        v = jnp.where(right, v, pltpu.roll(v, 0, 1, stride=1, stride_axis=0))
        pixels = jnp.zeros((1, W), F32)
        for k in range(W // BLOCK_COLS):
            pixels = jnp.where(line == k, valid[r, k].astype(F32), pixels)
        corr[r] = (v * pixels).astype(BF)
    side = 1 - parity()
    even[...] = corr[pl.ds(side, 3)]
    odd[...] = corr[pl.ds(1 - side, 3)]
    even_out[...] = even_c[...]
    odd_out[...] = odd_c[...]


def gate_kernel(a, token, out):
    out[...] = a[...]


def volume_kernel(
    corr, even, odd, carried, pick, w1, w2, w3, w4, p1, p2, p3, ph, im, ie,
    pre2, pre3, main, ah, ae,
    ext, cs, h1, h2, h3, acc, comb, a1, a2, a3, am,
):
    place_weights(w1, w2, w3, w4, p1, p2, p3, ph, im, ie, a1, a2, a3, ah, am, ae)
    disp = corr.shape[1]
    bands = lax.axis_size("rows")
    me = lax.axis_index("rows")
    side = 1 - parity()
    top_live = (me > 0).astype(F32)
    bottom_live = (me < bands - 1).astype(F32)

    ext[:, 0:8, :] = jnp.zeros((10, 8, W), F32)
    ext[:, pl.ds(8 + disp, 8), :] = jnp.zeros((10, 8, W), F32)
    ext[3:7, pl.ds(8, disp), :] = corr[...].astype(F32)
    ext[pl.ds(7 * side, 3), pl.ds(8, disp), :] = even[...].astype(F32)
    ext[pl.ds(7 * (1 - side), 3), pl.ds(8, disp), :] = odd[...].astype(F32)
    starts = window_starts(disp)
    lane = lanes((16, W))
    for k, d0 in enumerate(starts):
        cs[k, 480:512, :] = jnp.zeros((32, W), BF)
        for r in range(10):
            v = ext[r, d0 + 7 : d0 + 23, :]
            low = jnp.where(lane == 0, 0.0, pltpu.roll(v, 1, 1))
            high = jnp.where(lane == W - 1, 0.0, pltpu.roll(v, W - 1, 1))
            cs[k, r * 48 : r * 48 + 16, :] = low.astype(BF)
            cs[k, r * 48 + 16 : r * 48 + 32, :] = v.astype(BF)
            cs[k, r * 48 + 32 : r * 48 + 48, :] = high.astype(BF)

    zero_row = jnp.zeros((8, A, W), BF)
    h1[0] = zero_row
    h1[disp + 1] = zero_row
    h2[0] = zero_row[:R]
    h2[disp + 1] = zero_row[:R]

    w1 = a1[...]
    for k, d0 in enumerate(starts):
        x = jnp.concatenate([cs[k, pl.ds(j * 48, 256), :] for j in (0, 3, 5)], axis=1)
        p = jnp.maximum(dot(w1, x), 0.0)
        for g, j0 in enumerate((0, 3, 5)):
            q = p[:, g * W : (g + 1) * W].reshape(T1, 3, A, W)
            for t in range(3):
                j = j0 + t
                if g == 2 and t == 0:
                    continue
                v = q[:, t]
                if j < 2:
                    v = v * top_live
                if j > 5:
                    v = v * bottom_live
                h1[pl.ds(1 + d0, T1), j] = v.astype(BF)

    w2 = a2[...]
    sel = pick[...]

    for i in range(disp // 4):
        c = carried[:, pl.ds(i * 16, 16), :].reshape(256, W)
        own = dot(sel, c)
        for g in range(3):
            x = jnp.concatenate(
                [h1[pl.ds(4 * i + 2 * h, 4), 2 * g : 2 * g + 4].reshape(256, W) for h in range(2)], axis=1
            )
            p = dot(w2, x)
            for h in range(2):
                for d in range(2):
                    for r in range(2):
                        n = (d * 2 + r) * 48
                        v = combine(p[n : n + 48, h * W : (h + 1) * W])
                        j = 2 * g + r
                        dd = 2 * h + d
                        if j == 0:
                            pre2[0, 4 * i + dd] = v
                        elif j == 5:
                            pre2[1, 4 * i + dd] = v
                        else:
                            m = (dd * R + j - 1) * A
                            v = jnp.maximum(v + own[m : m + A], 0.0)
                            h2[4 * i + dd + 1, j - 1] = v.astype(BF)

    w3 = a3[...]

    for i in range(disp // 4):
        x = jnp.concatenate([h2[pl.ds(4 * i + 2 * h, 4)].reshape(256, W) for h in range(2)], axis=1)
        p = dot(w3, x)
        for h in range(2):
            for d in range(2):
                for r in range(R):
                    n = (d * R + r) * 48
                    v = combine(p[n : n + 48, h * W : (h + 1) * W])
                    dd = 4 * i + 2 * h + d
                    if r == 0:
                        pre3[0, dd] = v
                    elif r == R - 1:
                        pre3[1, dd] = v
                    else:
                        h3[dd, r - 1] = jnp.maximum(v, 0.0).astype(BF)

    acc[0:2] = jnp.zeros((2, 24, W), F32)
    w4 = am[...]
    for k in range(disp // 8):
        p = dot(w4, h3[8 * k : 8 * k + 8].reshape(256, W)).reshape(10, 24, W)
        acc[8 * k : 8 * k + 2] += p[:2]
        acc[8 * k + 2 : 8 * k + 10] = p[2:]
    sum_columns(acc, comb, disp)
    for r in range(R):
        main[r] = comb[pl.ds(r + 1, disp, stride=8), :] + corr[r].astype(F32)


def sum_columns(acc, comb, disp):
    for d in range(disp):
        comb[d * 8 : d * 8 + 8, :] = shifted_sum(acc[d + 1, 0:8], acc[d + 1, 8:16], acc[d + 1, 16:24])


def edge_rows(side, carried, pre2, pre3, ah, ae, acc, h2, h3, comb):
    disp = carried.shape[0]
    me = lax.axis_index("rows")
    live = jnp.where(side == 0, me > 0, me < lax.axis_size("rows") - 1).astype(F32)
    zero_row = jnp.zeros((A, W), BF)
    h2[0] = zero_row
    h2[disp + 1] = zero_row
    v = jnp.maximum(pre2[...] + carried[...].astype(F32), 0.0) * live
    h2[1 : disp + 1] = v.astype(BF)
    w3 = ah[side]
    for d0 in window_starts(disp):
        p = dot(w3, h2[d0 : d0 + 16].reshape(256, W))
        for d in range(T1):
            v = combine(p[d * 48 : d * 48 + 48]) + pre3[d0 + d]
            h3[d0 + d] = jnp.maximum(v, 0.0).astype(BF)
    w4 = ae[side]
    acc[0:2] = jnp.zeros((2, 24, W), F32)
    for k in range(disp // 16):
        p = dot(w4, h3[16 * k : 16 * k + 16].reshape(256, W)).reshape(18, 24, W)
        acc[16 * k : 16 * k + 2] += p[:2]
        acc[16 * k + 2 : 16 * k + 18] = p[2:]
    sum_columns(acc, comb, disp)


def first_kernel(carried, main_in, pre2, pre3, ah, ae, main, part, pre2_rest, pre3_rest, acc, h2, h3, comb):
    disp = carried.shape[0]
    side = parity()
    edge_rows(side, carried, pre2.at[side], pre3.at[side], ah, ae, acc, h2, h3, comb)
    part[...] = comb[pl.ds(5 * side, disp, stride=8), :].astype(BF)
    for r in range(R):
        v = main_in[r] + jnp.where(side == r // 2, comb[pl.ds(r + 1, disp, stride=8), :], 0.0)
        main[pl.ds(r, disp, stride=R), :] = v
    pre2_rest[...] = pre2[1 - side]
    pre3_rest[...] = pre3[1 - side]


def last_kernel(carried, main_in, pre2, pre3, ah, ae, main, part, acc, h2, h3, comb):
    disp = carried.shape[0]
    side = 1 - parity()
    main[...] = main_in[...]
    edge_rows(side, carried, pre2, pre3, ah, ae, acc, h2, h3, comb)
    part[...] = comb[pl.ds(5 * side, disp, stride=8), :].astype(BF)
    for k in range(2):
        r = 2 * side + k
        main[pl.ds(r, disp, stride=R), :] += comb[pl.ds(r + 1, disp, stride=8), :]


def add_kernel(main, odd, even, out):
    disp = odd.shape[0]
    out[...] = main[...]
    side = parity()
    for k, part in enumerate((odd, even)):
        edge = side if k == 0 else 1 - side
        out[pl.ds((R - 1) * edge, disp, stride=R), :] += part[...].astype(F32)


def call(kernel, outs, args, specs=None, scratch=(), sems=0, us=2.0):
    return pl.pallas_call(
        kernel,
        out_shape=tuple(jax.ShapeDtypeStruct(s, d) for s, d in outs),
        in_specs=specs or [VM] * len(args),
        out_specs=tuple(VM for _ in outs),
        scratch_shapes=[pltpu.VMEM(s, d) for s, d in scratch] + [pltpu.SemaphoreType.DMA((sems,))] * (sems > 0),
        compiler_params=pltpu.CompilerParams(vmem_limit_bytes=24 * MIB),
        cost_estimate=pl.CostEstimate(flops=int(us * 1.1e9), bytes_accessed=1000, transcendentals=0),
    )(*args)


def local(features, partner, pattern, valid, carried, w_first, w_second, w_third, w_last):
    channels = features.shape[1]
    disp = carried.shape[2]
    bands = lax.axis_size("rows")
    cams = lax.axis_size("cam")
    even_pairs = [p for k in range(0, bands - 1, 2) for p in ((k, k + 1), (k + 1, k))]
    odd_pairs = [p for k in range(1, bands - 1, 2) for p in ((k, k + 1), (k + 1, k))]

    def swap(x, pairs):
        return lax.ppermute(x, "rows", pairs)

    own = features.reshape(channels * R, W)
    mate = lax.ppermute(own, "cam", [(i, i ^ 1) for i in range(cams)])
    flat = carried.reshape(A, disp * R, W)
    edge = ((disp, A, W), BF)
    even_c, odd_c = call(edges_kernel, [edge, edge], [flat], us=EDGES)
    rows3 = ((3, disp, W), BF)
    corr, even_r, odd_r, even_c, odd_c = call(
        corr_kernel,
        [((R, disp, W), BF), rows3, rows3, edge, edge],
        [own, mate, partner, pattern, valid[0], even_c, odd_c],
        specs=[VM, VM, SM, SM, SM, VM, VM],
        us=CORR,
    )
    odd_r = swap(odd_r, odd_pairs)
    odd_c = swap(odd_c, odd_pairs)
    even_r = swap(even_r, even_pairs)
    even_c = swap(even_c, even_pairs)

    by_tap = lambda w: w.transpose(1, 2, 0).reshape(A * A, 27)
    ie = np.stack([place_last([0], 16), place_last([R - 1], 16)])
    consts = [place_first(), place_second(), place_third(), place_halo(), place_last([1, 2], 8), ie]
    far = [flat, bf(pick_carried().reshape(256, 256)), w_first.T, by_tap(w_second), by_tap(w_third), w_last.T]
    far += [bf(c) for c in consts]
    pre = ((2, disp, A, W), F32)
    rows = ((R, disp, W), F32)
    line = ((disp, W), BF)
    pre2, pre3, main, ah, ae = call(
        volume_kernel,
        [pre, pre, rows, ((2, T1 * 48, 256), BF), ((2, 432, 256), BF)],
        [corr, even_r, odd_r] + far,
        scratch=[
            ((10, disp + 16, W), F32),
            ((len(window_starts(disp)), 512, W), BF),
            ((disp + 2, 8, A, W), BF),
            ((disp + 2, R, A, W), BF),
            ((disp, 2, A, W), BF),
            ((disp + 2, 24, W), F32),
            ((disp * 8, W), F32),
            ((T1 * 48, 256), BF),
            ((192, 256), BF),
            ((384, 256), BF),
            ((240, 256), BF),
        ]
        ,us=VOL,
    )
    scratch = [
        ((disp + 2, 24, W), F32),
        ((disp + 2, A, W), BF),
        ((disp, A, W), BF),
        ((disp * 8, W), F32),
    ]
    half = ((disp, A, W), F32)
    flat_rows = ((disp * R, W), F32)
    main, odd_part, pre2, pre3 = call(
        first_kernel, [flat_rows, line, half, half], [odd_c, main, pre2, pre3, ah, ae], scratch=scratch, us=EDGE
    )
    odd_part = swap(odd_part, odd_pairs)
    main, even_part = call(
        last_kernel, [flat_rows, line], [even_c, main, pre2, pre3, ah, ae], scratch=scratch, us=EDGE
    )
    even_part = swap(even_part, even_pairs)
    (out,) = call(add_kernel, [flat_rows], [main, odd_part, even_part], us=0.1)
    return out.reshape(1, disp, R, W)


def solution(mesh):
    return jax.shard_map(
        local,
        mesh=mesh,
        in_specs=(
            P(("seg", "cam"), None, "rows", None),
            P(),
            P(("seg", "rows"), None),
            P(("seg", "cam"), "rows", None),
            P(("seg", "cam"), None, None, "rows", None),
            P(),
            P(),
            P(),
            P(),
        ),
        out_specs=P(("seg", "cam"), None, "rows", None),
        check_vma=False,
    )
```

```python
import numpy as np
import jax
import jax.numpy as jnp
from jax import lax
from jax.experimental import pallas as pl
from jax.experimental.pallas import tpu as pltpu
from jax.sharding import PartitionSpec as P

DTILE = 16
BLOCK_COLS = 32
BF = jnp.bfloat16
F32 = jnp.float32
VM = pl.BlockSpec(memory_space=pltpu.VMEM)
SM = pl.BlockSpec(memory_space=pltpu.SMEM)
HB = pl.BlockSpec(memory_space=pltpu.HBM)
MIB = 2**20
EDGES, CORR, VOL, EDGE = 1.5, 1.5, 8.0, 2.0

R, W, A = 4, 128, 16
T1 = 14


def window_starts(disp):
    count = -(-disp // T1)
    return [min(T1 * k, disp - T1) for k in range(count)]


def place_first():
    m = np.zeros((27, T1 * 3, 256), np.float32)
    for d in range(T1):
        for r in range(3):
            for a in range(3):
                for b in range(3):
                    for e in range(3):
                        col = (r + b) * 48 + e * 16 + d + a
                        m[9 * a + 3 * b + e, d * 3 + r, col] = 1
    return m.reshape(27, -1)


def place_second():
    m = np.zeros((3, 3, A, 2, 2, 4, 4, A), np.float32)
    c = np.arange(A)
    for d in range(2):
        for r in range(2):
            for a in range(3):
                for b in range(3):
                    m[a, b, c, d, r, d + a, r + b, c] = 1
    return m.reshape(9 * A, 4 * 256)


def place_third():
    m = np.zeros((3, 3, A, 2, R, 4, R, A), np.float32)
    c = np.arange(A)
    for d in range(2):
        for r in range(R):
            for a in range(3):
                for b in range(3):
                    if 0 <= r + b - 1 < R:
                        m[a, b, c, d, r, d + a, r + b - 1, c] = 1
    return m.reshape(9 * A, 2 * R * 256)


def place_halo():
    m = np.zeros((3, A, T1, 16, A), np.float32)
    c = np.arange(A)
    for d in range(T1):
        for a in range(3):
            m[a, c, d, d + a, c] = 1
    return m.reshape(3 * A, T1 * 256)


def place_last(rows, depth):
    n = len(rows)
    m = np.zeros((depth + 2, 3, 8, depth, n, 27), np.float32)
    for d in range(depth):
        for k, r in enumerate(rows):
            for a in range(3):
                for b in range(3):
                    for e in range(3):
                        m[d - (a - 1) + 1, e, r - (b - 1) + 1, d, k, 9 * a + 3 * b + e] = 1
    return m.reshape((depth + 2) * 24, depth * n * 27)


def pick_carried():
    m = np.zeros((4, R, A, A, 4, R), np.float32)
    for d in range(4):
        for r in range(R):
            for o in range(A):
                m[d, r, o, o, d, r] = 1
    return m


def bf(x):
    return jnp.asarray(x, BF)


def dot(a, b):
    return jnp.dot(a, b, preferred_element_type=F32)


def lanes(shape):
    return lax.broadcasted_iota(jnp.int32, shape, len(shape) - 1)


def shifted_sum(low, mid, high):
    lane = lanes(mid.shape)
    low = jnp.where(lane == 0, 0.0, pltpu.roll(low, 1, low.ndim - 1))
    high = jnp.where(lane == W - 1, 0.0, pltpu.roll(high, W - 1, high.ndim - 1))
    return mid + low + high


def combine(p):
    return shifted_sum(p[0:A], p[A : 2 * A], p[2 * A : 3 * A])


def parity():
    return lax.rem(lax.axis_index("rows"), 2)


def edge_pick(row):
    m = lax.broadcasted_iota(jnp.int32, (4 * A, 256), 0)
    n = lax.broadcasted_iota(jnp.int32, (4 * A, 256), 1)
    want = (m % A) * 16 + (m // A) * R + row
    return jnp.where(n == want, 1.0, 0.0).astype(BF)


def edges_kernel(carried, even, odd):
    last = R - 1
    even_row = jnp.where(parity() == 0, last, 0)
    both = jnp.concatenate([edge_pick(even_row), edge_pick(last - even_row)], axis=0)
    for q in range(carried.shape[1] // 16):
        v = dot(both, carried[:, q * 16 : q * 16 + 16, :].reshape(256, W)).astype(BF)
        even[4 * q : 4 * q + 4] = v[:64].reshape(4, A, W)
        odd[4 * q : 4 * q + 4] = v[64:].reshape(4, A, W)


def ordered(w):
    outs = []
    v = w[...]
    for e in range(3):
        t = lax.broadcasted_iota(jnp.int32, (27, 9 * A), 0)
        n = lax.broadcasted_iota(jnp.int32, (27, 9 * A), 1)
        take = jnp.where(t == (n // A) * 3 + e, 1.0, 0.0).astype(BF)
        spread = dot(v, take)
        m = lax.broadcasted_iota(jnp.int32, spread.shape, 0)
        n = lax.broadcasted_iota(jnp.int32, spread.shape, 1)
        spread = jnp.where(m % A == n % A, spread, 0.0).astype(BF)
        o = lax.broadcasted_iota(jnp.int32, (A, A * A), 0)
        m = lax.broadcasted_iota(jnp.int32, (A, A * A), 1)
        gather = jnp.where(m // A == o, 1.0, 0.0).astype(BF)
        outs.append(dot(gather, spread).astype(BF))
    return jnp.concatenate(outs, axis=0)


def place_weights(w1, w2, w3, w4, p1, p2, p3, ph, im, ie, a1, a2, a3, ah, am, ae):
    v = dot(w1[...], p1[...]).astype(BF)
    for k in range(3 * T1):
        a1[pl.ds(k * A, A), :] = v[:, k * 256 : (k + 1) * 256]
    v = dot(ordered(w2), p2[...]).astype(BF)
    for k in range(4):
        a2[pl.ds(k * 48, 48), :] = v[:, k * 256 : (k + 1) * 256]
    third = ordered(w3)
    v = dot(third, p3[...]).astype(BF)
    for k in range(2 * R):
        a3[pl.ds(k * 48, 48), :] = v[:, k * 256 : (k + 1) * 256]
    for side in range(2):
        v = dot(ah_source(third, side), ph[...]).astype(BF)
        for k in range(T1):
            ah[side, pl.ds(k * 48, 48), :] = v[:, k * 256 : (k + 1) * 256]
    m = lax.broadcasted_iota(jnp.int32, (432, 27), 0)
    n = lax.broadcasted_iota(jnp.int32, (432, 27), 1)
    tall = jnp.where(m % 27 == n, 1.0, 0.0).astype(BF)
    tall = lax.dot_general(tall, w4[...], (((1,), (1,)), ((), ())), preferred_element_type=F32).astype(BF)
    m = lax.broadcasted_iota(jnp.int32, (A, 256), 0)
    n = lax.broadcasted_iota(jnp.int32, (A, 256), 1)
    wide = jnp.where(n % A == m, 1.0, 0.0).astype(BF)
    blocks = dot(tall, wide)
    m = lax.broadcasted_iota(jnp.int32, (432, 256), 0)
    n = lax.broadcasted_iota(jnp.int32, (432, 256), 1)
    blocks = jnp.where(m // 27 == n // A, blocks, 0.0).astype(BF)
    am[...] = dot(im[...], blocks).astype(BF)
    for side in range(2):
        ae[side] = dot(ie[side], blocks).astype(BF)


def ah_source(w3, side):
    b = 2 * side
    return jnp.concatenate([w3[:, (3 * a + b) * A : (3 * a + b + 1) * A] for a in range(3)], axis=1)


def corr_kernel(own, mate, partner, pattern, valid, even_c, odd_c, corr, even, odd, even_out, odd_out):
    cam = lax.axis_index("cam")
    right = partner[cam] < cam
    line = lanes((1, W)) // BLOCK_COLS
    disp = corr.shape[1]
    channels = own.shape[0] // R
    x, y = own[...], mate[...]
    left_side = jnp.where(right, x, y)
    right_side = jnp.where(right, y, x)
    lane = lanes((W, W))
    sub = lax.broadcasted_iota(jnp.int32, (W, W), 0)
    flip = jnp.where(lane + sub == W - 1, 1.0, 0.0).astype(BF)
    lt = dot(left_side, flip).astype(BF).T
    row = lax.rem(lax.broadcasted_iota(jnp.int32, right_side.shape, 0), R)
    zero = jnp.zeros((), BF)
    rs = jnp.concatenate([jnp.where(row == r, right_side, zero) for r in range(R)], axis=1)
    s = dot(lt, rs)
    scale = 1.0 / np.sqrt(channels).astype(np.float32)
    for r in range(R):
        v = pltpu.roll(s[:, r * W : (r + 1) * W], 1, 1, stride=1, stride_axis=0)
        v = jnp.where(lane <= sub, v, 0.0).T[:disp] * scale
        v = jnp.concatenate(
            [v[t * DTILE : (t + 1) * DTILE] * pattern[r, t].astype(F32) for t in range(disp // DTILE)], axis=0
        )
        v = dot(v.astype(BF), flip)
        v = jnp.where(right, v, pltpu.roll(v, 0, 1, stride=1, stride_axis=0))
        pixels = jnp.zeros((1, W), F32)
        for k in range(W // BLOCK_COLS):
            pixels = jnp.where(line == k, valid[r, k].astype(F32), pixels)
        corr[r] = (v * pixels).astype(BF)
    side = 1 - parity()
    even[...] = corr[pl.ds(side, 3)]
    odd[...] = corr[pl.ds(1 - side, 3)]
    even_out[...] = even_c[...]
    odd_out[...] = odd_c[...]


def gate_kernel(a, token, out):
    out[...] = a[...]


def volume_kernel(
    corr, even, odd, carried, pick, w1, w2, w3, w4, p1, p2, p3, ph, im, ie,
    pre2, pre3, main, ah, ae,
    ext, cs, h1, h2, h3, acc, comb, a1, a2, a3, am,
):
    place_weights(w1, w2, w3, w4, p1, p2, p3, ph, im, ie, a1, a2, a3, ah, am, ae)
    disp = corr.shape[1]
    bands = lax.axis_size("rows")
    me = lax.axis_index("rows")
    side = 1 - parity()
    top_live = (me > 0).astype(F32)
    bottom_live = (me < bands - 1).astype(F32)

    ext[:, 0:8, :] = jnp.zeros((10, 8, W), F32)
    ext[:, pl.ds(8 + disp, 8), :] = jnp.zeros((10, 8, W), F32)
    ext[3:7, pl.ds(8, disp), :] = corr[...].astype(F32)
    ext[pl.ds(7 * side, 3), pl.ds(8, disp), :] = even[...].astype(F32)
    ext[pl.ds(7 * (1 - side), 3), pl.ds(8, disp), :] = odd[...].astype(F32)
    starts = window_starts(disp)
    lane = lanes((16, W))
    for k, d0 in enumerate(starts):
        cs[k, 480:512, :] = jnp.zeros((32, W), BF)
        for r in range(10):
            v = ext[r, d0 + 7 : d0 + 23, :]
            low = jnp.where(lane == 0, 0.0, pltpu.roll(v, 1, 1))
            high = jnp.where(lane == W - 1, 0.0, pltpu.roll(v, W - 1, 1))
            cs[k, r * 48 : r * 48 + 16, :] = low.astype(BF)
            cs[k, r * 48 + 16 : r * 48 + 32, :] = v.astype(BF)
            cs[k, r * 48 + 32 : r * 48 + 48, :] = high.astype(BF)

    zero_row = jnp.zeros((8, A, W), BF)
    h1[0] = zero_row
    h1[disp + 1] = zero_row
    h2[0] = zero_row[:R]
    h2[disp + 1] = zero_row[:R]

    w1 = a1[...]
    for k, d0 in enumerate(starts):
        x = jnp.concatenate([cs[k, pl.ds(j * 48, 256), :] for j in (0, 3, 5)], axis=1)
        p = jnp.maximum(dot(w1, x), 0.0)
        for g, j0 in enumerate((0, 3, 5)):
            q = p[:, g * W : (g + 1) * W].reshape(T1, 3, A, W)
            for t in range(3):
                j = j0 + t
                if g == 2 and t == 0:
                    continue
                v = q[:, t]
                if j < 2:
                    v = v * top_live
                if j > 5:
                    v = v * bottom_live
                h1[pl.ds(1 + d0, T1), j] = v.astype(BF)

    w2 = a2[...]
    sel = pick[...]

    for i in range(disp // 4):
        c = carried[:, pl.ds(i * 16, 16), :].reshape(256, W)
        own = dot(sel, c)
        for g in range(3):
            x = jnp.concatenate(
                [h1[pl.ds(4 * i + 2 * h, 4), 2 * g : 2 * g + 4].reshape(256, W) for h in range(2)], axis=1
            )
            p = dot(w2, x)
            for h in range(2):
                for d in range(2):
                    for r in range(2):
                        n = (d * 2 + r) * 48
                        v = combine(p[n : n + 48, h * W : (h + 1) * W])
                        j = 2 * g + r
                        dd = 2 * h + d
                        if j == 0:
                            pre2[0, 4 * i + dd] = v
                        elif j == 5:
                            pre2[1, 4 * i + dd] = v
                        else:
                            m = (dd * R + j - 1) * A
                            v = jnp.maximum(v + own[m : m + A], 0.0)
                            h2[4 * i + dd + 1, j - 1] = v.astype(BF)

    w3 = a3[...]

    for i in range(disp // 4):
        x = jnp.concatenate([h2[pl.ds(4 * i + 2 * h, 4)].reshape(256, W) for h in range(2)], axis=1)
        p = dot(w3, x)
        for h in range(2):
            for d in range(2):
                for r in range(R):
                    n = (d * R + r) * 48
                    v = combine(p[n : n + 48, h * W : (h + 1) * W])
                    dd = 4 * i + 2 * h + d
                    if r == 0:
                        pre3[0, dd] = v
                    elif r == R - 1:
                        pre3[1, dd] = v
                    else:
                        h3[dd, r - 1] = jnp.maximum(v, 0.0).astype(BF)

    acc[0:2] = jnp.zeros((2, 24, W), F32)
    w4 = am[...]
    for k in range(disp // 8):
        p = dot(w4, h3[8 * k : 8 * k + 8].reshape(256, W)).reshape(10, 24, W)
        acc[8 * k : 8 * k + 2] += p[:2]
        acc[8 * k + 2 : 8 * k + 10] = p[2:]
    sum_columns(acc, comb, disp)
    for r in range(R):
        main[r] = comb[pl.ds(r + 1, disp, stride=8), :] + corr[r].astype(F32)


def sum_columns(acc, comb, disp):
    for d in range(disp):
        comb[d * 8 : d * 8 + 8, :] = shifted_sum(acc[d + 1, 0:8], acc[d + 1, 8:16], acc[d + 1, 16:24])


def edge_rows(side, carried, pre2, pre3, ah, ae, acc, h2, h3, comb):
    disp = carried.shape[0]
    me = lax.axis_index("rows")
    live = jnp.where(side == 0, me > 0, me < lax.axis_size("rows") - 1).astype(F32)
    zero_row = jnp.zeros((A, W), BF)
    h2[0] = zero_row
    h2[disp + 1] = zero_row
    v = jnp.maximum(pre2[...] + carried[...].astype(F32), 0.0) * live
    h2[1 : disp + 1] = v.astype(BF)
    w3 = ah[side]
    for d0 in window_starts(disp):
        p = dot(w3, h2[d0 : d0 + 16].reshape(256, W))
        for d in range(T1):
            v = combine(p[d * 48 : d * 48 + 48]) + pre3[d0 + d]
            h3[d0 + d] = jnp.maximum(v, 0.0).astype(BF)
    w4 = ae[side]
    acc[0:2] = jnp.zeros((2, 24, W), F32)
    for k in range(disp // 16):
        p = dot(w4, h3[16 * k : 16 * k + 16].reshape(256, W)).reshape(18, 24, W)
        acc[16 * k : 16 * k + 2] += p[:2]
        acc[16 * k + 2 : 16 * k + 18] = p[2:]
    sum_columns(acc, comb, disp)


def first_kernel(carried, main_in, pre2, pre3, ah, ae, main, part, pre2_rest, pre3_rest, acc, h2, h3, comb):
    disp = carried.shape[0]
    side = parity()
    edge_rows(side, carried, pre2.at[side], pre3.at[side], ah, ae, acc, h2, h3, comb)
    part[:disp] = comb[pl.ds(5 * side, disp, stride=8), :]
    part[disp:] = jnp.zeros((part.shape[0] - disp, W), F32)
    for r in range(R):
        v = main_in[r] + jnp.where(side == r // 2, comb[pl.ds(r + 1, disp, stride=8), :], 0.0)
        main[pl.ds(r, disp, stride=R), :] = v
    pre2_rest[...] = pre2[1 - side]
    pre3_rest[...] = pre3[1 - side]


def last_kernel(carried, main_in, pre2, pre3, ah, ae, main, part, acc, h2, h3, comb):
    disp = carried.shape[0]
    side = 1 - parity()
    main[...] = main_in[...]
    edge_rows(side, carried, pre2, pre3, ah, ae, acc, h2, h3, comb)
    part[...] = comb[pl.ds(5 * side, disp, stride=8), :]
    for k in range(2):
        r = 2 * side + k
        main[pl.ds(r, disp, stride=R), :] += comb[pl.ds(r + 1, disp, stride=8), :]


def add_kernel(main, odd, even, out):
    disp = even.shape[0]
    out[...] = main[...]
    side = parity()
    for k, part in enumerate((odd, even)):
        edge = side if k == 0 else 1 - side
        out[pl.ds((R - 1) * edge, disp, stride=R), :] += part[:disp]


def call(kernel, outs, args, specs=None, scratch=(), sems=0, us=2.0):
    return pl.pallas_call(
        kernel,
        out_shape=tuple(jax.ShapeDtypeStruct(s, d) for s, d in outs),
        in_specs=specs or [VM] * len(args),
        out_specs=tuple(VM for _ in outs),
        scratch_shapes=[pltpu.VMEM(s, d) for s, d in scratch] + [pltpu.SemaphoreType.DMA((sems,))] * (sems > 0),
        compiler_params=pltpu.CompilerParams(vmem_limit_bytes=24 * MIB),
        cost_estimate=pl.CostEstimate(flops=int(us * 1.1e9), bytes_accessed=1000, transcendentals=0),
    )(*args)


def local(features, partner, pattern, valid, carried, w_first, w_second, w_third, w_last):
    channels = features.shape[1]
    disp = carried.shape[2]
    bands = lax.axis_size("rows")
    cams = lax.axis_size("cam")
    even_pairs = [p for k in range(0, bands - 1, 2) for p in ((k, k + 1), (k + 1, k))]
    odd_pairs = [p for k in range(1, bands - 1, 2) for p in ((k, k + 1), (k + 1, k))]

    def swap(x, pairs):
        return lax.ppermute(x, "rows", pairs)

    own = features.reshape(channels * R, W)
    mate = lax.ppermute(own, "cam", [(i, i ^ 1) for i in range(cams)])
    flat = carried.reshape(A, disp * R, W)
    edge = ((disp, A, W), BF)
    even_c, odd_c = call(edges_kernel, [edge, edge], [flat], us=EDGES)
    rows3 = ((3, disp, W), BF)
    corr, even_r, odd_r, even_c, odd_c = call(
        corr_kernel,
        [((R, disp, W), BF), rows3, rows3, edge, edge],
        [own, mate, partner, pattern, valid[0], even_c, odd_c],
        specs=[VM, VM, SM, SM, SM, VM, VM],
        us=CORR,
    )
    odd_r = swap(odd_r, odd_pairs)
    odd_c = swap(odd_c, odd_pairs)
    even_r = swap(even_r, even_pairs)
    even_c = swap(even_c, even_pairs)

    by_tap = lambda w: w.transpose(1, 2, 0).reshape(A * A, 27)
    ie = np.stack([place_last([0], 16), place_last([R - 1], 16)])
    consts = [place_first(), place_second(), place_third(), place_halo(), place_last([1, 2], 8), ie]
    far = [flat, bf(pick_carried().reshape(256, 256)), w_first.T, by_tap(w_second), by_tap(w_third), w_last.T]
    far += [bf(c) for c in consts]
    pre = ((2, disp, A, W), F32)
    rows = ((R, disp, W), F32)
    line = ((disp, W), F32)
    pre2, pre3, main, ah, ae = call(
        volume_kernel,
        [pre, pre, rows, ((2, T1 * 48, 256), BF), ((2, 432, 256), BF)],
        [corr, even_r, odd_r] + far,
        scratch=[
            ((10, disp + 16, W), F32),
            ((len(window_starts(disp)), 512, W), BF),
            ((disp + 2, 8, A, W), BF),
            ((disp + 2, R, A, W), BF),
            ((disp, 2, A, W), BF),
            ((disp + 2, 24, W), F32),
            ((disp * 8, W), F32),
            ((T1 * 48, 256), BF),
            ((192, 256), BF),
            ((384, 256), BF),
            ((240, 256), BF),
        ]
        ,us=VOL,
    )
    scratch = [
        ((disp + 2, 24, W), F32),
        ((disp + 2, A, W), BF),
        ((disp, A, W), BF),
        ((disp * 8, W), F32),
    ]
    half = ((disp, A, W), F32)
    flat_rows = ((disp * R, W), F32)
    main, odd_part, pre2, pre3 = call(
        first_kernel, [flat_rows, ((disp + 8, W), F32), half, half], [odd_c, main, pre2, pre3, ah, ae], scratch=scratch, us=EDGE
    )
    odd_part = swap(odd_part, odd_pairs)
    main, even_part = call(
        last_kernel, [flat_rows, line], [even_c, main, pre2, pre3, ah, ae], scratch=scratch, us=EDGE
    )
    even_part = swap(even_part, even_pairs)
    (out,) = call(add_kernel, [flat_rows], [main, odd_part, even_part], us=0.1)
    return out.reshape(1, disp, R, W)


def solution(mesh):
    return jax.shard_map(
        local,
        mesh=mesh,
        in_specs=(
            P(("seg", "cam"), None, "rows", None),
            P(),
            P(("seg", "rows"), None),
            P(("seg", "cam"), "rows", None),
            P(("seg", "cam"), None, None, "rows", None),
            P(),
            P(),
            P(),
            P(),
        ),
        out_specs=P(("seg", "cam"), None, "rows", None),
        check_vma=False,
    )
```

```python
import numpy as np
import jax
import jax.numpy as jnp
from jax import lax
from jax.experimental import pallas as pl
from jax.experimental.pallas import tpu as pltpu
from jax.sharding import PartitionSpec as P

DTILE = 16
BLOCK_COLS = 32
BF = jnp.bfloat16
F32 = jnp.float32
VM = pl.BlockSpec(memory_space=pltpu.VMEM)
SM = pl.BlockSpec(memory_space=pltpu.SMEM)
HB = pl.BlockSpec(memory_space=pltpu.HBM)
MIB = 2**20
EDGES, CORR, VOL, EDGE = 1.5, 1.5, 8.0, 2.0

R, W, A = 4, 128, 16
T1 = 14


def window_starts(disp):
    count = -(-disp // T1)
    return [min(T1 * k, disp - T1) for k in range(count)]


def place_first():
    m = np.zeros((27, T1 * 3, 256), np.float32)
    for d in range(T1):
        for r in range(3):
            for a in range(3):
                for b in range(3):
                    for e in range(3):
                        col = (r + b) * 48 + e * 16 + d + a
                        m[9 * a + 3 * b + e, d * 3 + r, col] = 1
    return m.reshape(27, -1)


def place_second():
    m = np.zeros((3, 3, A, 2, 2, 4, 4, A), np.float32)
    c = np.arange(A)
    for d in range(2):
        for r in range(2):
            for a in range(3):
                for b in range(3):
                    m[a, b, c, d, r, d + a, r + b, c] = 1
    return m.reshape(9 * A, 4 * 256)


def place_third():
    m = np.zeros((3, 3, A, 2, R, 4, R, A), np.float32)
    c = np.arange(A)
    for d in range(2):
        for r in range(R):
            for a in range(3):
                for b in range(3):
                    if 0 <= r + b - 1 < R:
                        m[a, b, c, d, r, d + a, r + b - 1, c] = 1
    return m.reshape(9 * A, 2 * R * 256)


def place_halo():
    m = np.zeros((3, A, T1, 16, A), np.float32)
    c = np.arange(A)
    for d in range(T1):
        for a in range(3):
            m[a, c, d, d + a, c] = 1
    return m.reshape(3 * A, T1 * 256)


def place_last(rows, depth):
    n = len(rows)
    m = np.zeros((depth + 2, 3, 8, depth, n, 27), np.float32)
    for d in range(depth):
        for k, r in enumerate(rows):
            for a in range(3):
                for b in range(3):
                    for e in range(3):
                        m[d - (a - 1) + 1, e, r - (b - 1) + 1, d, k, 9 * a + 3 * b + e] = 1
    return m.reshape((depth + 2) * 24, depth * n * 27)


def pick_carried():
    m = np.zeros((4, R, A, A, 4, R), np.float32)
    for d in range(4):
        for r in range(R):
            for o in range(A):
                m[d, r, o, o, d, r] = 1
    return m


def bf(x):
    return jnp.asarray(x, BF)


def dot(a, b):
    return jnp.dot(a, b, preferred_element_type=F32)


def lanes(shape):
    return lax.broadcasted_iota(jnp.int32, shape, len(shape) - 1)


def shifted_sum(low, mid, high):
    lane = lanes(mid.shape)
    low = jnp.where(lane == 0, 0.0, pltpu.roll(low, 1, low.ndim - 1))
    high = jnp.where(lane == W - 1, 0.0, pltpu.roll(high, W - 1, high.ndim - 1))
    return mid + low + high


def combine(p):
    return shifted_sum(p[0:A], p[A : 2 * A], p[2 * A : 3 * A])


def parity():
    return lax.rem(lax.axis_index("rows"), 2)


def edge_pick(row):
    m = lax.broadcasted_iota(jnp.int32, (4 * A, 256), 0)
    n = lax.broadcasted_iota(jnp.int32, (4 * A, 256), 1)
    want = (m % A) * 16 + (m // A) * R + row
    return jnp.where(n == want, 1.0, 0.0).astype(BF)


def edges_kernel(carried, even, odd):
    last = R - 1
    even_row = jnp.where(parity() == 0, last, 0)
    both = jnp.concatenate([edge_pick(even_row), edge_pick(last - even_row)], axis=0)
    for q in range(carried.shape[1] // 16):
        v = dot(both, carried[:, q * 16 : q * 16 + 16, :].reshape(256, W)).astype(BF)
        even[4 * q : 4 * q + 4] = v[:64].reshape(4, A, W)
        odd[4 * q : 4 * q + 4] = v[64:].reshape(4, A, W)


def ordered(w):
    outs = []
    v = w[...]
    for e in range(3):
        t = lax.broadcasted_iota(jnp.int32, (27, 9 * A), 0)
        n = lax.broadcasted_iota(jnp.int32, (27, 9 * A), 1)
        take = jnp.where(t == (n // A) * 3 + e, 1.0, 0.0).astype(BF)
        spread = dot(v, take)
        m = lax.broadcasted_iota(jnp.int32, spread.shape, 0)
        n = lax.broadcasted_iota(jnp.int32, spread.shape, 1)
        spread = jnp.where(m % A == n % A, spread, 0.0).astype(BF)
        o = lax.broadcasted_iota(jnp.int32, (A, A * A), 0)
        m = lax.broadcasted_iota(jnp.int32, (A, A * A), 1)
        gather = jnp.where(m // A == o, 1.0, 0.0).astype(BF)
        outs.append(dot(gather, spread).astype(BF))
    return jnp.concatenate(outs, axis=0)


def place_weights(w1, w2, w3, w4, p1, p2, p3, ph, im, ie, a1, a2, a3, ah, am, ae):
    v = dot(w1[...], p1[...]).astype(BF)
    for k in range(3 * T1):
        a1[pl.ds(k * A, A), :] = v[:, k * 256 : (k + 1) * 256]
    v = dot(ordered(w2), p2[...]).astype(BF)
    for k in range(4):
        a2[pl.ds(k * 48, 48), :] = v[:, k * 256 : (k + 1) * 256]
    third = ordered(w3)
    v = dot(third, p3[...]).astype(BF)
    for k in range(2 * R):
        a3[pl.ds(k * 48, 48), :] = v[:, k * 256 : (k + 1) * 256]
    for side in range(2):
        v = dot(ah_source(third, side), ph[...]).astype(BF)
        for k in range(T1):
            ah[side, pl.ds(k * 48, 48), :] = v[:, k * 256 : (k + 1) * 256]
    m = lax.broadcasted_iota(jnp.int32, (432, 27), 0)
    n = lax.broadcasted_iota(jnp.int32, (432, 27), 1)
    tall = jnp.where(m % 27 == n, 1.0, 0.0).astype(BF)
    tall = lax.dot_general(tall, w4[...], (((1,), (1,)), ((), ())), preferred_element_type=F32).astype(BF)
    m = lax.broadcasted_iota(jnp.int32, (A, 256), 0)
    n = lax.broadcasted_iota(jnp.int32, (A, 256), 1)
    wide = jnp.where(n % A == m, 1.0, 0.0).astype(BF)
    blocks = dot(tall, wide)
    m = lax.broadcasted_iota(jnp.int32, (432, 256), 0)
    n = lax.broadcasted_iota(jnp.int32, (432, 256), 1)
    blocks = jnp.where(m // 27 == n // A, blocks, 0.0).astype(BF)
    am[...] = dot(im[...], blocks).astype(BF)
    for side in range(2):
        ae[side] = dot(ie[side], blocks).astype(BF)


def ah_source(w3, side):
    b = 2 * side
    return jnp.concatenate([w3[:, (3 * a + b) * A : (3 * a + b + 1) * A] for a in range(3)], axis=1)


def corr_kernel(own, mate, partner, pattern, valid, even_c, odd_c, corr, even, odd, even_out, odd_out):
    cam = lax.axis_index("cam")
    right = partner[cam] < cam
    line = lanes((1, W)) // BLOCK_COLS
    disp = corr.shape[1]
    channels = own.shape[0] // R
    x, y = own[...], mate[...]
    left_side = jnp.where(right, x, y)
    right_side = jnp.where(right, y, x)
    lane = lanes((W, W))
    sub = lax.broadcasted_iota(jnp.int32, (W, W), 0)
    flip = jnp.where(lane + sub == W - 1, 1.0, 0.0).astype(BF)
    lt = dot(left_side, flip).astype(BF).T
    row = lax.rem(lax.broadcasted_iota(jnp.int32, right_side.shape, 0), R)
    zero = jnp.zeros((), BF)
    rs = jnp.concatenate([jnp.where(row == r, right_side, zero) for r in range(R)], axis=1)
    s = dot(lt, rs)
    scale = 1.0 / np.sqrt(channels).astype(np.float32)
    for r in range(R):
        v = pltpu.roll(s[:, r * W : (r + 1) * W], 1, 1, stride=1, stride_axis=0)
        v = jnp.where(lane <= sub, v, 0.0).T[:disp] * scale
        v = jnp.concatenate(
            [v[t * DTILE : (t + 1) * DTILE] * pattern[r, t].astype(F32) for t in range(disp // DTILE)], axis=0
        )
        v = dot(v.astype(BF), flip)
        v = jnp.where(right, v, pltpu.roll(v, 0, 1, stride=1, stride_axis=0))
        pixels = jnp.zeros((1, W), F32)
        for k in range(W // BLOCK_COLS):
            pixels = jnp.where(line == k, valid[r, k].astype(F32), pixels)
        corr[r] = (v * pixels).astype(BF)
    side = 1 - parity()
    even[...] = corr[pl.ds(side, 3)]
    odd[...] = corr[pl.ds(1 - side, 3)]
    even_out[...] = even_c[...]
    odd_out[...] = odd_c[...]


def gate_kernel(a, token, out):
    out[...] = a[...]


def volume_kernel(
    corr, even, odd, carried, pick, w1, w2, w3, w4, p1, p2, p3, ph, im, ie,
    pre2, pre3, main, ah, ae,
    ext, cs, h1, h2, h3, acc, comb, a1, a2, a3, am,
):
    place_weights(w1, w2, w3, w4, p1, p2, p3, ph, im, ie, a1, a2, a3, ah, am, ae)
    disp = corr.shape[1]
    bands = lax.axis_size("rows")
    me = lax.axis_index("rows")
    side = 1 - parity()
    top_live = (me > 0).astype(F32)
    bottom_live = (me < bands - 1).astype(F32)

    ext[:, 0:8, :] = jnp.zeros((10, 8, W), F32)
    ext[:, pl.ds(8 + disp, 8), :] = jnp.zeros((10, 8, W), F32)
    ext[3:7, pl.ds(8, disp), :] = corr[...].astype(F32)
    ext[pl.ds(7 * side, 3), pl.ds(8, disp), :] = even[...].astype(F32)
    ext[pl.ds(7 * (1 - side), 3), pl.ds(8, disp), :] = odd[...].astype(F32)
    starts = window_starts(disp)
    lane = lanes((16, W))
    for k, d0 in enumerate(starts):
        cs[k, 480:512, :] = jnp.zeros((32, W), BF)
        for r in range(10):
            v = ext[r, d0 + 7 : d0 + 23, :]
            low = jnp.where(lane == 0, 0.0, pltpu.roll(v, 1, 1))
            high = jnp.where(lane == W - 1, 0.0, pltpu.roll(v, W - 1, 1))
            cs[k, r * 48 : r * 48 + 16, :] = low.astype(BF)
            cs[k, r * 48 + 16 : r * 48 + 32, :] = v.astype(BF)
            cs[k, r * 48 + 32 : r * 48 + 48, :] = high.astype(BF)

    zero_row = jnp.zeros((8, A, W), BF)
    h1[0] = zero_row
    h1[disp + 1] = zero_row
    h2[0] = zero_row[:R]
    h2[disp + 1] = zero_row[:R]

    w1 = a1[...]
    for k, d0 in enumerate(starts):
        x = jnp.concatenate([cs[k, pl.ds(j * 48, 256), :] for j in (0, 3, 5)], axis=1)
        p = jnp.maximum(dot(w1, x), 0.0)
        for g, j0 in enumerate((0, 3, 5)):
            q = p[:, g * W : (g + 1) * W].reshape(T1, 3, A, W)
            for t in range(3):
                j = j0 + t
                if g == 2 and t == 0:
                    continue
                v = q[:, t]
                if j < 2:
                    v = v * top_live
                if j > 5:
                    v = v * bottom_live
                h1[pl.ds(1 + d0, T1), j] = v.astype(BF)

    w2 = a2[...]
    sel = pick[...]

    for i in range(disp // 4):
        c = carried[:, pl.ds(i * 16, 16), :].reshape(256, W)
        own = dot(sel, c)
        for g in range(3):
            x = jnp.concatenate(
                [h1[pl.ds(4 * i + 2 * h, 4), 2 * g : 2 * g + 4].reshape(256, W) for h in range(2)], axis=1
            )
            p = dot(w2, x)
            for h in range(2):
                for d in range(2):
                    for r in range(2):
                        n = (d * 2 + r) * 48
                        v = combine(p[n : n + 48, h * W : (h + 1) * W])
                        j = 2 * g + r
                        dd = 2 * h + d
                        if j == 0:
                            pre2[0, 4 * i + dd] = v
                        elif j == 5:
                            pre2[1, 4 * i + dd] = v
                        else:
                            m = (dd * R + j - 1) * A
                            v = jnp.maximum(v + own[m : m + A], 0.0)
                            h2[4 * i + dd + 1, j - 1] = v.astype(BF)

    w3 = a3[...]

    for i in range(disp // 4):
        x = jnp.concatenate([h2[pl.ds(4 * i + 2 * h, 4)].reshape(256, W) for h in range(2)], axis=1)
        p = dot(w3, x)
        for h in range(2):
            for d in range(2):
                for r in range(R):
                    n = (d * R + r) * 48
                    v = combine(p[n : n + 48, h * W : (h + 1) * W])
                    dd = 4 * i + 2 * h + d
                    if r == 0:
                        pre3[0, dd] = v
                    elif r == R - 1:
                        pre3[1, dd] = v
                    else:
                        h3[dd, r - 1] = jnp.maximum(v, 0.0).astype(BF)

    acc[0:2] = jnp.zeros((2, 24, W), F32)
    w4 = am[...]
    for k in range(disp // 8):
        p = dot(w4, h3[8 * k : 8 * k + 8].reshape(256, W)).reshape(10, 24, W)
        acc[8 * k : 8 * k + 2] += p[:2]
        acc[8 * k + 2 : 8 * k + 10] = p[2:]
    sum_columns(acc, comb, disp)
    for r in range(R):
        main[r] = comb[pl.ds(r + 1, disp, stride=8), :] + corr[r].astype(F32)


def sum_columns(acc, comb, disp):
    for d in range(disp):
        comb[d * 8 : d * 8 + 8, :] = shifted_sum(acc[d + 1, 0:8], acc[d + 1, 8:16], acc[d + 1, 16:24])


def edge_rows(side, carried, pre2, pre3, ah, ae, acc, h2, h3, comb):
    disp = carried.shape[0]
    me = lax.axis_index("rows")
    live = jnp.where(side == 0, me > 0, me < lax.axis_size("rows") - 1).astype(F32)
    zero_row = jnp.zeros((A, W), BF)
    h2[0] = zero_row
    h2[disp + 1] = zero_row
    v = jnp.maximum(pre2[...] + carried[...].astype(F32), 0.0) * live
    h2[1 : disp + 1] = v.astype(BF)
    w3 = ah[side]
    starts = window_starts(disp)
    for n in range(0, len(starts), 2):
        pair = starts[n : n + 2]
        p = dot(w3, jnp.concatenate([h2[d0 : d0 + 16].reshape(256, W) for d0 in pair], axis=1))
        for k, d0 in enumerate(pair):
            for d in range(T1):
                v = combine(p[d * 48 : d * 48 + 48, k * W : (k + 1) * W]) + pre3[d0 + d]
                h3[d0 + d] = jnp.maximum(v, 0.0).astype(BF)
    w4 = ae[side]
    acc[0:2] = jnp.zeros((2, 24, W), F32)
    for n in range(0, disp // 16, 2):
        x = jnp.concatenate([h3[16 * k : 16 * k + 16].reshape(256, W) for k in (n, n + 1)], axis=1)
        both = dot(w4, x)
        for k in (n, n + 1):
            p = both[:, (k - n) * W : (k - n + 1) * W].reshape(18, 24, W)
            acc[16 * k : 16 * k + 2] += p[:2]
            acc[16 * k + 2 : 16 * k + 18] = p[2:]
    sum_columns(acc, comb, disp)


def first_kernel(carried, main_in, pre2, pre3, ah, ae, main, part, pre2_rest, pre3_rest, acc, h2, h3, comb):
    disp = carried.shape[0]
    side = parity()
    edge_rows(side, carried, pre2.at[side], pre3.at[side], ah, ae, acc, h2, h3, comb)
    part[:disp] = comb[pl.ds(5 * side, disp, stride=8), :]
    part[disp:] = jnp.zeros((part.shape[0] - disp, W), F32)
    for r in range(R):
        v = main_in[r] + jnp.where(side == r // 2, comb[pl.ds(r + 1, disp, stride=8), :], 0.0)
        main[pl.ds(r, disp, stride=R), :] = v
    pre2_rest[...] = pre2[1 - side]
    pre3_rest[...] = pre3[1 - side]


def last_kernel(carried, main_in, pre2, pre3, ah, ae, main, part, acc, h2, h3, comb):
    disp = carried.shape[0]
    side = 1 - parity()
    main[...] = main_in[...]
    edge_rows(side, carried, pre2, pre3, ah, ae, acc, h2, h3, comb)
    part[...] = comb[pl.ds(5 * side, disp, stride=8), :]
    for k in range(2):
        r = 2 * side + k
        main[pl.ds(r, disp, stride=R), :] += comb[pl.ds(r + 1, disp, stride=8), :]


def add_kernel(main, odd, even, out):
    disp = even.shape[0]
    out[...] = main[...]
    side = parity()
    for k, part in enumerate((odd, even)):
        edge = side if k == 0 else 1 - side
        out[pl.ds((R - 1) * edge, disp, stride=R), :] += part[:disp]


def call(kernel, outs, args, specs=None, scratch=(), sems=0, us=2.0):
    return pl.pallas_call(
        kernel,
        out_shape=tuple(jax.ShapeDtypeStruct(s, d) for s, d in outs),
        in_specs=specs or [VM] * len(args),
        out_specs=tuple(VM for _ in outs),
        scratch_shapes=[pltpu.VMEM(s, d) for s, d in scratch] + [pltpu.SemaphoreType.DMA((sems,))] * (sems > 0),
        compiler_params=pltpu.CompilerParams(vmem_limit_bytes=24 * MIB),
        cost_estimate=pl.CostEstimate(flops=int(us * 1.1e9), bytes_accessed=1000, transcendentals=0),
    )(*args)


def local(features, partner, pattern, valid, carried, w_first, w_second, w_third, w_last):
    channels = features.shape[1]
    disp = carried.shape[2]
    bands = lax.axis_size("rows")
    cams = lax.axis_size("cam")
    even_pairs = [p for k in range(0, bands - 1, 2) for p in ((k, k + 1), (k + 1, k))]
    odd_pairs = [p for k in range(1, bands - 1, 2) for p in ((k, k + 1), (k + 1, k))]

    def swap(x, pairs):
        return lax.ppermute(x, "rows", pairs)

    own = features.reshape(channels * R, W)
    mate = lax.ppermute(own, "cam", [(i, i ^ 1) for i in range(cams)])
    flat = carried.reshape(A, disp * R, W)
    edge = ((disp, A, W), BF)
    even_c, odd_c = call(edges_kernel, [edge, edge], [flat], us=EDGES)
    rows3 = ((3, disp, W), BF)
    corr, even_r, odd_r, even_c, odd_c = call(
        corr_kernel,
        [((R, disp, W), BF), rows3, rows3, edge, edge],
        [own, mate, partner, pattern, valid[0], even_c, odd_c],
        specs=[VM, VM, SM, SM, SM, VM, VM],
        us=CORR,
    )
    odd_r = swap(odd_r, odd_pairs)
    odd_c = swap(odd_c, odd_pairs)
    even_r = swap(even_r, even_pairs)
    even_c = swap(even_c, even_pairs)

    by_tap = lambda w: w.transpose(1, 2, 0).reshape(A * A, 27)
    ie = np.stack([place_last([0], 16), place_last([R - 1], 16)])
    consts = [place_first(), place_second(), place_third(), place_halo(), place_last([1, 2], 8), ie]
    far = [flat, bf(pick_carried().reshape(256, 256)), w_first.T, by_tap(w_second), by_tap(w_third), w_last.T]
    far += [bf(c) for c in consts]
    pre = ((2, disp, A, W), F32)
    rows = ((R, disp, W), F32)
    line = ((disp, W), F32)
    pre2, pre3, main, ah, ae = call(
        volume_kernel,
        [pre, pre, rows, ((2, T1 * 48, 256), BF), ((2, 432, 256), BF)],
        [corr, even_r, odd_r] + far,
        scratch=[
            ((10, disp + 16, W), F32),
            ((len(window_starts(disp)), 512, W), BF),
            ((disp + 2, 8, A, W), BF),
            ((disp + 2, R, A, W), BF),
            ((disp, 2, A, W), BF),
            ((disp + 2, 24, W), F32),
            ((disp * 8, W), F32),
            ((T1 * 48, 256), BF),
            ((192, 256), BF),
            ((384, 256), BF),
            ((240, 256), BF),
        ]
        ,us=VOL,
    )
    scratch = [
        ((disp + 2, 24, W), F32),
        ((disp + 2, A, W), BF),
        ((disp, A, W), BF),
        ((disp * 8, W), F32),
    ]
    half = ((disp, A, W), F32)
    flat_rows = ((disp * R, W), F32)
    main, odd_part, pre2, pre3 = call(
        first_kernel, [flat_rows, ((disp + 8, W), F32), half, half], [odd_c, main, pre2, pre3, ah, ae], scratch=scratch, us=EDGE
    )
    odd_part = swap(odd_part, odd_pairs)
    main, even_part = call(
        last_kernel, [flat_rows, line], [even_c, main, pre2, pre3, ah, ae], scratch=scratch, us=EDGE
    )
    even_part = swap(even_part, even_pairs)
    (out,) = call(add_kernel, [flat_rows], [main, odd_part, even_part], us=0.1)
    return out.reshape(1, disp, R, W)


def solution(mesh):
    return jax.shard_map(
        local,
        mesh=mesh,
        in_specs=(
            P(("seg", "cam"), None, "rows", None),
            P(),
            P(("seg", "rows"), None),
            P(("seg", "cam"), "rows", None),
            P(("seg", "cam"), None, None, "rows", None),
            P(),
            P(),
            P(),
            P(),
        ),
        out_specs=P(("seg", "cam"), None, "rows", None),
        check_vma=False,
    )
```

```python
import numpy as np
import jax
import jax.numpy as jnp
from jax import lax
from jax.experimental import pallas as pl
from jax.experimental.pallas import tpu as pltpu
from jax.sharding import PartitionSpec as P

DTILE = 16
BLOCK_COLS = 32
BF = jnp.bfloat16
F32 = jnp.float32
VM = pl.BlockSpec(memory_space=pltpu.VMEM)
SM = pl.BlockSpec(memory_space=pltpu.SMEM)
HB = pl.BlockSpec(memory_space=pltpu.HBM)
MIB = 2**20
EDGES, CORR, VOL, EDGE = 1.5, 1.5, 8.0, 2.0

R, W, A = 4, 128, 16
T1 = 14


def window_starts(disp):
    count = -(-disp // T1)
    return [min(T1 * k, disp - T1) for k in range(count)]


def place_first():
    m = np.zeros((27, T1 * 3, 256), np.float32)
    for d in range(T1):
        for r in range(3):
            for a in range(3):
                for b in range(3):
                    for e in range(3):
                        col = (r + b) * 48 + e * 16 + d + a
                        m[9 * a + 3 * b + e, d * 3 + r, col] = 1
    return m.reshape(27, -1)


def place_second():
    m = np.zeros((3, 3, A, 2, 2, 4, 4, A), np.float32)
    c = np.arange(A)
    for d in range(2):
        for r in range(2):
            for a in range(3):
                for b in range(3):
                    m[a, b, c, d, r, d + a, r + b, c] = 1
    return m.reshape(9 * A, 4 * 256)


def place_third():
    m = np.zeros((3, 3, A, 2, R, 4, R, A), np.float32)
    c = np.arange(A)
    for d in range(2):
        for r in range(R):
            for a in range(3):
                for b in range(3):
                    if 0 <= r + b - 1 < R:
                        m[a, b, c, d, r, d + a, r + b - 1, c] = 1
    return m.reshape(9 * A, 2 * R * 256)


def place_halo():
    m = np.zeros((3, A, T1, 16, A), np.float32)
    c = np.arange(A)
    for d in range(T1):
        for a in range(3):
            m[a, c, d, d + a, c] = 1
    return m.reshape(3 * A, T1 * 256)


def place_last(rows, depth):
    n = len(rows)
    m = np.zeros((depth + 2, 3, 8, depth, n, 27), np.float32)
    for d in range(depth):
        for k, r in enumerate(rows):
            for a in range(3):
                for b in range(3):
                    for e in range(3):
                        m[d - (a - 1) + 1, e, r - (b - 1) + 1, d, k, 9 * a + 3 * b + e] = 1
    return m.reshape((depth + 2) * 24, depth * n * 27)


def pick_carried():
    m = np.zeros((4, R, A, A, 4, R), np.float32)
    for d in range(4):
        for r in range(R):
            for o in range(A):
                m[d, r, o, o, d, r] = 1
    return m


def bf(x):
    return jnp.asarray(x, BF)


def dot(a, b):
    return jnp.dot(a, b, preferred_element_type=F32)


def lanes(shape):
    return lax.broadcasted_iota(jnp.int32, shape, len(shape) - 1)


def shifted_sum(low, mid, high):
    lane = lanes(mid.shape)
    low = jnp.where(lane == 0, 0.0, pltpu.roll(low, 1, low.ndim - 1))
    high = jnp.where(lane == W - 1, 0.0, pltpu.roll(high, W - 1, high.ndim - 1))
    return mid + low + high


def combine(p):
    return shifted_sum(p[0:A], p[A : 2 * A], p[2 * A : 3 * A])


def parity():
    return lax.rem(lax.axis_index("rows"), 2)


def edge_pick(row):
    m = lax.broadcasted_iota(jnp.int32, (4 * A, 256), 0)
    n = lax.broadcasted_iota(jnp.int32, (4 * A, 256), 1)
    want = (m % A) * 16 + (m // A) * R + row
    return jnp.where(n == want, 1.0, 0.0).astype(BF)


def edges_kernel(carried, even, odd):
    last = R - 1
    even_row = jnp.where(parity() == 0, last, 0)
    both = jnp.concatenate([edge_pick(even_row), edge_pick(last - even_row)], axis=0)
    for n in range(0, carried.shape[1] // 16, 2):
        x = jnp.concatenate([carried[:, q * 16 : q * 16 + 16, :].reshape(256, W) for q in (n, n + 1)], axis=1)
        p = dot(both, x).astype(BF)
        for q in (n, n + 1):
            v = p[:, (q - n) * W : (q - n + 1) * W]
            even[4 * q : 4 * q + 4] = v[:64].reshape(4, A, W)
            odd[4 * q : 4 * q + 4] = v[64:].reshape(4, A, W)


def ordered(w):
    outs = []
    v = w[...]
    for e in range(3):
        t = lax.broadcasted_iota(jnp.int32, (27, 9 * A), 0)
        n = lax.broadcasted_iota(jnp.int32, (27, 9 * A), 1)
        take = jnp.where(t == (n // A) * 3 + e, 1.0, 0.0).astype(BF)
        spread = dot(v, take)
        m = lax.broadcasted_iota(jnp.int32, spread.shape, 0)
        n = lax.broadcasted_iota(jnp.int32, spread.shape, 1)
        spread = jnp.where(m % A == n % A, spread, 0.0).astype(BF)
        o = lax.broadcasted_iota(jnp.int32, (A, A * A), 0)
        m = lax.broadcasted_iota(jnp.int32, (A, A * A), 1)
        gather = jnp.where(m // A == o, 1.0, 0.0).astype(BF)
        outs.append(dot(gather, spread).astype(BF))
    return jnp.concatenate(outs, axis=0)


def place_weights(w1, w2, w3, w4, p1, p2, p3, ph, im, ie, a1, a2, a3, ah, am, ae):
    v = dot(w1[...], p1[...]).astype(BF)
    for k in range(3 * T1):
        a1[pl.ds(k * A, A), :] = v[:, k * 256 : (k + 1) * 256]
    v = dot(ordered(w2), p2[...]).astype(BF)
    for k in range(4):
        a2[pl.ds(k * 48, 48), :] = v[:, k * 256 : (k + 1) * 256]
    third = ordered(w3)
    v = dot(third, p3[...]).astype(BF)
    for k in range(2 * R):
        a3[pl.ds(k * 48, 48), :] = v[:, k * 256 : (k + 1) * 256]
    for side in range(2):
        v = dot(ah_source(third, side), ph[...]).astype(BF)
        for k in range(T1):
            ah[side, pl.ds(k * 48, 48), :] = v[:, k * 256 : (k + 1) * 256]
    m = lax.broadcasted_iota(jnp.int32, (432, 27), 0)
    n = lax.broadcasted_iota(jnp.int32, (432, 27), 1)
    tall = jnp.where(m % 27 == n, 1.0, 0.0).astype(BF)
    tall = lax.dot_general(tall, w4[...], (((1,), (1,)), ((), ())), preferred_element_type=F32).astype(BF)
    m = lax.broadcasted_iota(jnp.int32, (A, 256), 0)
    n = lax.broadcasted_iota(jnp.int32, (A, 256), 1)
    wide = jnp.where(n % A == m, 1.0, 0.0).astype(BF)
    blocks = dot(tall, wide)
    m = lax.broadcasted_iota(jnp.int32, (432, 256), 0)
    n = lax.broadcasted_iota(jnp.int32, (432, 256), 1)
    blocks = jnp.where(m // 27 == n // A, blocks, 0.0).astype(BF)
    am[...] = dot(im[...], blocks).astype(BF)
    for side in range(2):
        ae[side] = dot(ie[side], blocks).astype(BF)


def ah_source(w3, side):
    b = 2 * side
    return jnp.concatenate([w3[:, (3 * a + b) * A : (3 * a + b + 1) * A] for a in range(3)], axis=1)


def corr_kernel(own, mate, partner, pattern, valid, even_c, odd_c, corr, even, odd, even_out, odd_out):
    cam = lax.axis_index("cam")
    mates = jnp.broadcast_to(partner[...].astype(F32), (1, partner.shape[1]))
    flag = jnp.zeros((1, W), F32)
    for k in range(partner.shape[1]):
        one = jnp.broadcast_to(mates[:, k : k + 1], (1, W))
        flag = jnp.where(cam == k, one, flag)
    right = flag < cam.astype(F32)
    line = lanes((1, W)) // BLOCK_COLS
    disp = corr.shape[1]
    channels = own.shape[0] // R
    x, y = own[...], mate[...]
    left_side = jnp.where(right, x, y)
    right_side = jnp.where(right, y, x)
    lane = lanes((W, W))
    sub = lax.broadcasted_iota(jnp.int32, (W, W), 0)
    flip = jnp.where(lane + sub == W - 1, 1.0, 0.0).astype(BF)
    lt = dot(left_side, flip).astype(BF).T
    row = lax.rem(lax.broadcasted_iota(jnp.int32, right_side.shape, 0), R)
    zero = jnp.zeros((), BF)
    rs = jnp.concatenate([jnp.where(row == r, right_side, zero) for r in range(R)], axis=1)
    s = dot(lt, rs)
    scale = 1.0 / np.sqrt(channels).astype(np.float32)
    rows = []
    for r in range(R):
        v = pltpu.roll(s[:, r * W : (r + 1) * W], 1, 1, stride=1, stride_axis=0)
        v = jnp.where(lane <= sub, v, 0.0).T[:disp] * scale
        v = jnp.concatenate(
            [v[t * DTILE : (t + 1) * DTILE] * pattern[r : r + 1, t : t + 1].astype(F32) for t in range(disp // DTILE)], axis=0
        )
        rows.append(v.astype(BF))
    flipped = dot(jnp.concatenate(rows, axis=0), flip)
    for r in range(R):
        v = flipped[r * disp : (r + 1) * disp]
        v = jnp.where(right, v, pltpu.roll(v, 0, 1, stride=1, stride_axis=0))
        pixels = jnp.zeros((1, W), F32)
        for k in range(W // BLOCK_COLS):
            pixels = jnp.where(line == k, valid[r : r + 1, k : k + 1].astype(F32), pixels)
        corr[r] = (v * pixels).astype(BF)
    side = 1 - parity()
    even[...] = corr[pl.ds(side, 3)]
    odd[...] = corr[pl.ds(1 - side, 3)]
    even_out[...] = even_c[...]
    odd_out[...] = odd_c[...]


def gate_kernel(a, token, out):
    out[...] = a[...]


def volume_kernel(
    corr, even, odd, carried, pick, w1, w2, w3, w4, p1, p2, p3, ph, im, ie,
    pre2, pre3, main, ah, ae,
    ext, cs, h1, h2, h3, acc, comb, a1, a2, a3, am,
):
    place_weights(w1, w2, w3, w4, p1, p2, p3, ph, im, ie, a1, a2, a3, ah, am, ae)
    disp = corr.shape[1]
    bands = lax.axis_size("rows")
    me = lax.axis_index("rows")
    side = 1 - parity()
    top_live = (me > 0).astype(F32)
    bottom_live = (me < bands - 1).astype(F32)

    ext[:, 0:8, :] = jnp.zeros((10, 8, W), F32)
    ext[:, pl.ds(8 + disp, 8), :] = jnp.zeros((10, 8, W), F32)
    ext[3:7, pl.ds(8, disp), :] = corr[...].astype(F32)
    ext[pl.ds(7 * side, 3), pl.ds(8, disp), :] = even[...].astype(F32)
    ext[pl.ds(7 * (1 - side), 3), pl.ds(8, disp), :] = odd[...].astype(F32)
    starts = window_starts(disp)
    lane = lanes((16, W))
    for k, d0 in enumerate(starts):
        cs[k, 480:512, :] = jnp.zeros((32, W), BF)
        for r in range(10):
            v = ext[r, d0 + 7 : d0 + 23, :]
            low = jnp.where(lane == 0, 0.0, pltpu.roll(v, 1, 1))
            high = jnp.where(lane == W - 1, 0.0, pltpu.roll(v, W - 1, 1))
            cs[k, r * 48 : r * 48 + 16, :] = low.astype(BF)
            cs[k, r * 48 + 16 : r * 48 + 32, :] = v.astype(BF)
            cs[k, r * 48 + 32 : r * 48 + 48, :] = high.astype(BF)

    zero_row = jnp.zeros((8, A, W), BF)
    h1[0] = zero_row
    h1[disp + 1] = zero_row
    h2[0] = zero_row[:R]
    h2[disp + 1] = zero_row[:R]

    w1 = a1[...]
    for k, d0 in enumerate(starts):
        x = jnp.concatenate([cs[k, pl.ds(j * 48, 256), :] for j in (0, 3, 5)], axis=1)
        p = jnp.maximum(dot(w1, x), 0.0)
        for g, j0 in enumerate((0, 3, 5)):
            q = p[:, g * W : (g + 1) * W].reshape(T1, 3, A, W)
            for t in range(3):
                j = j0 + t
                if g == 2 and t == 0:
                    continue
                v = q[:, t]
                if j < 2:
                    v = v * top_live
                if j > 5:
                    v = v * bottom_live
                h1[pl.ds(1 + d0, T1), j] = v.astype(BF)

    w2 = a2[...]
    sel = pick[...]

    for i in range(disp // 4):
        c = carried[:, pl.ds(i * 16, 16), :].reshape(256, W)
        own = dot(sel, c)
        for g in range(3):
            x = jnp.concatenate(
                [h1[pl.ds(4 * i + 2 * h, 4), 2 * g : 2 * g + 4].reshape(256, W) for h in range(2)], axis=1
            )
            p = dot(w2, x)
            for h in range(2):
                for d in range(2):
                    for r in range(2):
                        n = (d * 2 + r) * 48
                        v = combine(p[n : n + 48, h * W : (h + 1) * W])
                        j = 2 * g + r
                        dd = 2 * h + d
                        if j == 0:
                            pre2[0, 4 * i + dd] = v
                        elif j == 5:
                            pre2[1, 4 * i + dd] = v
                        else:
                            m = (dd * R + j - 1) * A
                            v = jnp.maximum(v + own[m : m + A], 0.0)
                            h2[4 * i + dd + 1, j - 1] = v.astype(BF)

    w3 = a3[...]

    for i in range(disp // 4):
        x = jnp.concatenate([h2[pl.ds(4 * i + 2 * h, 4)].reshape(256, W) for h in range(2)], axis=1)
        p = dot(w3, x)
        for h in range(2):
            for d in range(2):
                for r in range(R):
                    n = (d * R + r) * 48
                    v = combine(p[n : n + 48, h * W : (h + 1) * W])
                    dd = 4 * i + 2 * h + d
                    if r == 0:
                        pre3[0, dd] = v
                    elif r == R - 1:
                        pre3[1, dd] = v
                    else:
                        h3[dd, r - 1] = jnp.maximum(v, 0.0).astype(BF)

    acc[0:2] = jnp.zeros((2, 24, W), F32)
    w4 = am[...]
    for k in range(disp // 8):
        p = dot(w4, h3[8 * k : 8 * k + 8].reshape(256, W)).reshape(10, 24, W)
        acc[8 * k : 8 * k + 2] += p[:2]
        acc[8 * k + 2 : 8 * k + 10] = p[2:]
    sum_columns(acc, comb, disp)
    for r in range(R):
        main[r] = comb[pl.ds(r + 1, disp, stride=8), :] + corr[r].astype(F32)


def sum_columns(acc, comb, disp):
    for d in range(disp):
        comb[d * 8 : d * 8 + 8, :] = shifted_sum(acc[d + 1, 0:8], acc[d + 1, 8:16], acc[d + 1, 16:24])


def edge_rows(side, carried, pre2, pre3, ah, ae, acc, h2, h3, comb):
    disp = carried.shape[0]
    me = lax.axis_index("rows")
    live = jnp.where(side == 0, me > 0, me < lax.axis_size("rows") - 1).astype(F32)
    zero_row = jnp.zeros((A, W), BF)
    h2[0] = zero_row
    h2[disp + 1] = zero_row
    v = jnp.maximum(pre2[...] + carried[...].astype(F32), 0.0) * live
    h2[1 : disp + 1] = v.astype(BF)
    w3 = ah[side]
    starts = window_starts(disp)
    for n in range(0, len(starts), 2):
        pair = starts[n : n + 2]
        p = dot(w3, jnp.concatenate([h2[d0 : d0 + 16].reshape(256, W) for d0 in pair], axis=1))
        for k, d0 in enumerate(pair):
            for d in range(T1):
                v = combine(p[d * 48 : d * 48 + 48, k * W : (k + 1) * W]) + pre3[d0 + d]
                h3[d0 + d] = jnp.maximum(v, 0.0).astype(BF)
    w4 = ae[side]
    acc[0:2] = jnp.zeros((2, 24, W), F32)
    for n in range(0, disp // 16, 2):
        x = jnp.concatenate([h3[16 * k : 16 * k + 16].reshape(256, W) for k in (n, n + 1)], axis=1)
        both = dot(w4, x)
        for k in (n, n + 1):
            p = both[:, (k - n) * W : (k - n + 1) * W].reshape(18, 24, W)
            acc[16 * k : 16 * k + 2] += p[:2]
            acc[16 * k + 2 : 16 * k + 18] = p[2:]
    sum_columns(acc, comb, disp)


def first_kernel(carried, main_in, pre2, pre3, ah, ae, main, part, pre2_rest, pre3_rest, acc, h2, h3, comb):
    disp = carried.shape[0]
    side = parity()
    edge_rows(side, carried, pre2.at[side], pre3.at[side], ah, ae, acc, h2, h3, comb)
    part[:disp] = comb[pl.ds(5 * side, disp, stride=8), :]
    part[disp:] = jnp.zeros((part.shape[0] - disp, W), F32)
    for r in range(R):
        v = main_in[r] + jnp.where(side == r // 2, comb[pl.ds(r + 1, disp, stride=8), :], 0.0)
        main[pl.ds(r, disp, stride=R), :] = v
    pre2_rest[...] = pre2[1 - side]
    pre3_rest[...] = pre3[1 - side]


def last_kernel(carried, main_in, pre2, pre3, ah, ae, main, part, acc, h2, h3, comb):
    disp = carried.shape[0]
    side = 1 - parity()
    main[...] = main_in[...]
    edge_rows(side, carried, pre2, pre3, ah, ae, acc, h2, h3, comb)
    part[...] = comb[pl.ds(5 * side, disp, stride=8), :]
    for k in range(2):
        r = 2 * side + k
        main[pl.ds(r, disp, stride=R), :] += comb[pl.ds(r + 1, disp, stride=8), :]


def add_kernel(main, odd, even, out):
    disp = even.shape[0]
    out[...] = main[...]
    side = parity()
    for k, part in enumerate((odd, even)):
        edge = side if k == 0 else 1 - side
        out[pl.ds((R - 1) * edge, disp, stride=R), :] += part[:disp]


def call(kernel, outs, args, specs=None, scratch=(), sems=0, us=2.0):
    return pl.pallas_call(
        kernel,
        out_shape=tuple(jax.ShapeDtypeStruct(s, d) for s, d in outs),
        in_specs=specs or [VM] * len(args),
        out_specs=tuple(VM for _ in outs),
        scratch_shapes=[pltpu.VMEM(s, d) for s, d in scratch] + [pltpu.SemaphoreType.DMA((sems,))] * (sems > 0),
        compiler_params=pltpu.CompilerParams(vmem_limit_bytes=24 * MIB),
        cost_estimate=pl.CostEstimate(flops=int(us * 1.1e9), bytes_accessed=1000, transcendentals=0),
    )(*args)


def local(features, partner, pattern, valid, carried, w_first, w_second, w_third, w_last):
    channels = features.shape[1]
    disp = carried.shape[2]
    bands = lax.axis_size("rows")
    cams = lax.axis_size("cam")
    even_pairs = [p for k in range(0, bands - 1, 2) for p in ((k, k + 1), (k + 1, k))]
    odd_pairs = [p for k in range(1, bands - 1, 2) for p in ((k, k + 1), (k + 1, k))]

    def swap(x, pairs):
        return lax.ppermute(x, "rows", pairs)

    own = features.reshape(channels * R, W)
    mate = lax.ppermute(own, "cam", [(i, i ^ 1) for i in range(cams)])
    flat = carried.reshape(A, disp * R, W)
    edge = ((disp, A, W), BF)
    even_c, odd_c = call(edges_kernel, [edge, edge], [flat], us=EDGES)
    rows3 = ((3, disp, W), BF)
    corr, even_r, odd_r, even_c, odd_c = call(
        corr_kernel,
        [((R, disp, W), BF), rows3, rows3, edge, edge],
        [own, mate, partner[None], pattern, valid[0], even_c, odd_c],
        specs=[VM] * 7,
        us=CORR,
    )
    odd_r = swap(odd_r, odd_pairs)
    odd_c = swap(odd_c, odd_pairs)
    even_r = swap(even_r, even_pairs)
    even_c = swap(even_c, even_pairs)

    by_tap = lambda w: w.transpose(1, 2, 0).reshape(A * A, 27)
    ie = np.stack([place_last([0], 16), place_last([R - 1], 16)])
    consts = [place_first(), place_second(), place_third(), place_halo(), place_last([1, 2], 8), ie]
    far = [flat, bf(pick_carried().reshape(256, 256)), w_first.T, by_tap(w_second), by_tap(w_third), w_last.T]
    far += [bf(c) for c in consts]
    pre = ((2, disp, A, W), F32)
    rows = ((R, disp, W), F32)
    line = ((disp, W), F32)
    pre2, pre3, main, ah, ae = call(
        volume_kernel,
        [pre, pre, rows, ((2, T1 * 48, 256), BF), ((2, 432, 256), BF)],
        [corr, even_r, odd_r] + far,
        scratch=[
            ((10, disp + 16, W), F32),
            ((len(window_starts(disp)), 512, W), BF),
            ((disp + 2, 8, A, W), BF),
            ((disp + 2, R, A, W), BF),
            ((disp, 2, A, W), BF),
            ((disp + 2, 24, W), F32),
            ((disp * 8, W), F32),
            ((T1 * 48, 256), BF),
            ((192, 256), BF),
            ((384, 256), BF),
            ((240, 256), BF),
        ]
        ,us=VOL,
    )
    scratch = [
        ((disp + 2, 24, W), F32),
        ((disp + 2, A, W), BF),
        ((disp, A, W), BF),
        ((disp * 8, W), F32),
    ]
    half = ((disp, A, W), F32)
    flat_rows = ((disp * R, W), F32)
    main, odd_part, pre2, pre3 = call(
        first_kernel, [flat_rows, ((disp + 8, W), F32), half, half], [odd_c, main, pre2, pre3, ah, ae], scratch=scratch, us=EDGE
    )
    odd_part = swap(odd_part, odd_pairs)
    main, even_part = call(
        last_kernel, [flat_rows, line], [even_c, main, pre2, pre3, ah, ae], scratch=scratch, us=EDGE
    )
    even_part = swap(even_part, even_pairs)
    (out,) = call(add_kernel, [flat_rows], [main, odd_part, even_part], us=0.1)
    return out.reshape(1, disp, R, W)


def solution(mesh):
    return jax.shard_map(
        local,
        mesh=mesh,
        in_specs=(
            P(("seg", "cam"), None, "rows", None),
            P(),
            P(("seg", "rows"), None),
            P(("seg", "cam"), "rows", None),
            P(("seg", "cam"), None, None, "rows", None),
            P(),
            P(),
            P(),
            P(),
        ),
        out_specs=P(("seg", "cam"), None, "rows", None),
        check_vma=False,
    )
```
